32 devices in a mesh: groups: 2 (over y), pair: 4 (over z), aux: 4 (over x, core).
Axes of the slice: x: 2, y: 2, z: 4, core: 2. Of those that a mesh axis runs over, the one named last changes fastest.
Arguments:
- panels: bfloat16 [128, 48, 768], P(('groups', 'pair')), parts along dimension 0, may hold values from -4 to 4
- amplitudes: bfloat16 [128, 2304], P(('groups', 'pair')), parts along dimension 0, may hold values from -4 to 4
- fitted_ints: bfloat16 [128, 2, 512, 768], P(('groups', 'pair'), None, 'aux'), parts along dimension 0, may hold values from -4 to 4
- pno_energy: float32 [128, 48], P(('groups', 'pair')), parts along dimension 0, may hold values from 0.3 to 3
- fock_occ: float32 [128, 64], P('groups'), parts along dimension 0, may hold values from -2.3 to 2.3, as said below
- pno_count: int32 [128], P(('groups', 'pair')), parts along dimension 0, may hold values from 12 to 48, as said below
- pair_pos: int32 [128], P('groups'), parts along dimension 0, may hold values from 0 to 63, as said below
- coupling: int32 [128, 28, 2], P('groups'), parts along dimension 0, may hold values from 0 to 63, as said below
- coupling_lmo: int32 [128, 28], P('groups'), parts along dimension 0, may hold values from 0 to 63
- pair_lmo: int32 [128, 2], P('groups'), parts along dimension 0, may hold values from 0 to 63
Outputs:
- residual: float32 [128, 2304], P(('groups', 'pair', 'aux')), parts along dimension 0
The draws below stay inside these ranges and needn't reach their ends.
There are 2 independent parts, one for each index of `groups`. The reference program is written for one: setup_inputs(seed, part) draws one part's arguments, and reference() takes and returns one part's arrays. A program takes and returns all parts, laid end to end along the dimension named above; each array names one. Nothing has to cross between parts.
Inputs may be any that keep to these rules, and one draw needn't show every extreme that they name: `pair_pos`: a permutation: every position once. `coupling`: for the 4 consecutive positions of one device in the output, the 224 pairs they name lie at most 56 on one pair index, and exactly 56 on some pair index. `pno_count`: some pair uses all 48. `fock_occ`: symmetric.
All inputs are finite; a program needn't handle non-finite values.
Results may differ from the reference program's by a relative error of at most 0.0037.
Values may be sent and summed in bfloat16 or wider, within the bound.
No kernel may reach another device: no remote copies, remote signals or barrier semaphores. Data moves between devices by JAX's collectives and lax.ppermute only.
A program may use at most 128 MiB of HBM per device.

```python
import jax
import jax.numpy as jnp
from jax import lax

PNO = 48
W = 768
NAUX = 512
NOCC = 64
NCPL = 28
PPD = 16
PAIRS = 64
PPA = 4
REQ = 224
CAP = 56
N_PAIR = 4


def coupling_tables(key):
    key_pos, key_cell, key_local = jax.random.split(key, 3)
    positions = jax.random.permutation(key_pos, PAIRS).astype(jnp.int32)
    label_at = jnp.argsort(positions, stable=True).astype(jnp.int32)
    block_total = PAIRS // PPA
    cell_keys = jax.random.split(key_cell, block_total)

    def pick_cells(cell_key):
        return jax.random.permutation(cell_key, N_PAIR * CAP)[:REQ]
    cell_ids = jax.vmap(pick_cells)(cell_keys).astype(jnp.int32)
    owner_dev = cell_ids // CAP
    local_pair = jax.random.randint(key_local, (block_total, REQ), 0, PPD).astype(jnp.int32)
    target = (owner_dev * PPD + local_pair).reshape(PAIRS, NCPL, 2)
    labels = jnp.take(label_at, target, axis=0).astype(jnp.int32)
    return (positions, labels)


def draw_pair_pos(key, part):
    tables = coupling_tables(key)
    return tables[0]


def draw_coupling(key, part):
    tables = coupling_tables(key)
    return tables[1]


def draw_panels(key, part):
    key = jax.random.fold_in(key, 11)
    key_basis, key_mixing, key_noise = jax.random.split(key, 3)
    basis_rows = jax.random.normal(key_basis, (PNO, W), jnp.float32)
    mixing = jax.random.normal(key_mixing, (PAIRS, PNO, PNO), jnp.float32)
    noise_part = jax.random.normal(key_noise, (PAIRS, PNO, W), jnp.float32)
    basis_rows = basis_rows / jnp.sqrt(float(W))
    mixing = mixing / jnp.sqrt(float(PNO))
    noise_part = noise_part / jnp.sqrt(float(W))
    shared = jnp.einsum('pab,bw->paw', mixing, basis_rows, precision=lax.Precision.HIGHEST)
    return jnp.clip(0.8 * shared + 0.6 * noise_part, -4.0, 4.0).astype(jnp.bfloat16)


def draw_fock_occ(key, part):
    key = jax.random.fold_in(key, 23)
    key_offdiag, key_diagonal = jax.random.split(key, 2)
    offdiag = jnp.clip(jax.random.normal(key_offdiag, (NOCC, NOCC), jnp.float32), -4.0, 4.0)
    offdiag = 0.4 * 0.7071 * (offdiag + offdiag.T)
    diagonal = jax.random.uniform(key_diagonal, (NOCC,), jnp.float32, -1.2, -0.3)
    identity = jnp.eye(NOCC, dtype=jnp.bool_)
    return jnp.where(identity, diagonal[:, None] * jnp.ones((1, NOCC), jnp.float32), offdiag)


def draw_pno_count(key, part):
    key = jax.random.fold_in(key, 37)
    key_count, key_full = jax.random.split(key, 2)
    counts = jax.random.randint(key_count, (PAIRS,), 12, PNO + 1).astype(jnp.int32)
    full_pair = jax.random.randint(key_full, (), 0, PAIRS).astype(jnp.int32)
    return jnp.where(jnp.arange(PAIRS, dtype=jnp.int32) == full_pair, PNO, counts).astype(jnp.int32)


def place_ends(entries, key, smallest, high):
    shape = entries.shape
    spot = [jax.random.randint(jax.random.fold_in(key, axis), (), 0, shape[axis]) for axis in range(len(shape))]
    entries = entries.at[tuple(spot)].set(smallest)
    longest = shape.index(max(shape))
    spot[longest] = (spot[longest] + 1) % shape[longest]
    return entries.at[tuple(spot)].set(high)


def strengthened(array, own_key, source, target, blocks, factor):
    owner, partner = [(jnp.arange(array.shape[position]) // (array.shape[position] // blocks)).reshape([-1 if axis == position else 1 for axis in range(array.ndim)]) for position in (source, target)]
    chosen = jax.random.permutation(own_key, blocks)[partner]
    strong = (owner == chosen) | (owner == (partner + blocks // 2) % blocks)
    return jnp.where(strong, factor * array, array)


def shard_levels(rng, extent, cuts, smallest, high):
    factor_of = 1.0
    for position, blocks in cuts:
        draws = jax.random.uniform(jax.random.fold_in(jax.random.fold_in(rng, 6), position), (blocks,), jnp.float32, smallest / len(cuts), high / len(cuts))
        factor_of = factor_of * jnp.repeat(jnp.exp(draws), extent[position] // blocks).reshape((-1,) + (1,) * (len(extent) - 1 - position))
    return factor_of


def gaussian(stream_key, shape, width, limit, cuts=(), held_as=jnp.bfloat16):
    result = jax.random.normal(stream_key, shape, jnp.float32) * width
    if len(cuts) > 0:
        result = shard_levels(stream_key, shape, cuts, -0.22, 0.18) * result
    return jnp.clip(result, min=-limit, max=limit).astype(held_as)


def noise_with(rng, extent, spread, limit, shards, heavy, held_as=jnp.bfloat16):
    values = spread * jax.random.normal(rng, extent, jnp.float32)
    if shards:
        values = values * shard_levels(rng, extent, shards, -0.22, 0.18)
    return jnp.clip(strengthened(values, jax.random.fold_in(rng, 3), *heavy), -limit, limit).astype(held_as)


def setup_inputs(seed: int = 0, part: int = 0) -> dict:
    keys = jax.random.split(jax.random.key(seed), 11)
    own_keys = jax.random.split(jax.random.fold_in(keys[10], part), 11)
    panels = draw_panels(jax.random.fold_in(jax.random.fold_in(keys[10], part), 71), part)
    amplitudes = gaussian(own_keys[1], (PAIRS, PNO * PNO), 0.3, 4.0, ((0, 4),))
    fitted_ints = noise_with(own_keys[2], (PAIRS, 2, NAUX, W), 0.2, 4.0, ((0, 4), (2, 4)), (2, 0, 4, 2.0))
    pno_energy = jnp.clip(0.3 + 2.7 * jax.random.uniform(own_keys[3], (PAIRS, PNO), jnp.float32) ** shard_levels(own_keys[3], (PAIRS, PNO), ((0, 4),), -0.2, 0.2), 0.3, 3.0)
    fock_occ = draw_fock_occ(jax.random.fold_in(jax.random.fold_in(keys[10], part), 71), part)
    pno_count = draw_pno_count(jax.random.fold_in(jax.random.fold_in(keys[10], part), 71), part)
    pair_pos = draw_pair_pos(jax.random.fold_in(jax.random.fold_in(keys[10], part), 71), part)
    coupling = draw_coupling(jax.random.fold_in(jax.random.fold_in(keys[10], part), 71), part)
    coupling_lmo = place_ends(jax.random.randint(own_keys[8], (PAIRS, NCPL), 0, NOCC), jax.random.fold_in(own_keys[8], 1), 0, NOCC - 1).astype(jnp.int32)
    pair_lmo = place_ends(jax.random.randint(own_keys[9], (PAIRS, 2), 0, NOCC), jax.random.fold_in(own_keys[9], 1), 0, NOCC - 1).astype(jnp.int32)
    return {"panels": panels, "amplitudes": amplitudes, "fitted_ints": fitted_ints, "pno_energy": pno_energy, "fock_occ": fock_occ, "pno_count": pno_count, "pair_pos": pair_pos, "coupling": coupling, "coupling_lmo": coupling_lmo, "pair_lmo": pair_lmo}


def round_half(values):
    return lax.optimization_barrier(values.astype(jnp.bfloat16)).astype(jnp.float32)


def reference(panels, amplitudes, fitted_ints, pno_energy, fock_occ, pno_count, pair_pos, coupling, coupling_lmo, pair_lmo):
    highest = lax.Precision.HIGHEST
    pair_total, pno_width, pao_width = panels.shape
    live_rows = jnp.arange(pno_width, dtype=jnp.int32)[None, :] < pno_count[:, None]
    masked_panels = jnp.where(live_rows[:, :, None], panels, jnp.zeros_like(panels))
    live_block = (live_rows[:, :, None] & live_rows[:, None, :]).reshape(pair_total, pno_width * pno_width)
    masked_amps = jnp.where(live_block, amplitudes, jnp.zeros_like(amplitudes))
    target = jnp.take(pair_pos, coupling, axis=0).astype(jnp.int32)

    def exchange_one(pair_item):
        fit_pair, panel = pair_item
        fitted = round_half(jnp.einsum('hqw,aw->hqa', fit_pair.astype(jnp.float32), panel.astype(jnp.float32), precision=highest))
        return jnp.einsum('qa,qb->ab', fitted[0], fitted[1], precision=highest).reshape(-1)

    exchange_k = lax.map(exchange_one, (fitted_ints, masked_panels))

    def couple_one(pair_item):
        panel, target_row, k_row, lmo_row = pair_item
        flat_target = target_row.reshape(-1)
        far_panels = jnp.take(masked_panels, flat_target, axis=0).astype(jnp.float32)
        far_amps = jnp.take(masked_amps, flat_target, axis=0).astype(jnp.float32).reshape(-1, pno_width, pno_width)
        intersection = round_half(jnp.einsum('aw,rbw->rab', panel.astype(jnp.float32), far_panels, precision=highest))
        half_product = round_half(jnp.einsum('rab,rbc->rac', intersection, far_amps, precision=highest))
        coupled = jnp.einsum('rac,rdc->rad', half_product, intersection, precision=highest)
        weight_left = fock_occ[k_row, lmo_row[1]]
        weight_right = fock_occ[lmo_row[0], k_row]
        weight = jnp.stack([weight_left, weight_right], axis=1).reshape(-1)
        return jnp.einsum('r,rab->ab', weight, coupled, precision=highest).reshape(-1)

    coupling_sum = lax.map(couple_one, (masked_panels, target, coupling_lmo, pair_lmo))
    occ_diag = jnp.diagonal(fock_occ)
    occ_pair = occ_diag[pair_lmo[:, 0]] + occ_diag[pair_lmo[:, 1]]
    energy_gap = pno_energy[:, :, None] + pno_energy[:, None, :] - occ_pair[:, None, None]
    diag_term = energy_gap.reshape(pair_total, -1) * masked_amps.astype(jnp.float32)
    total = exchange_k + diag_term - coupling_sum
    return jnp.where(live_block, total, jnp.zeros_like(total))
```

```python
import functools

import jax
import jax.numpy as jnp
from jax import lax
from jax.experimental import pallas as pl
from jax.experimental.pallas import tpu as pltpu
from jax.sharding import PartitionSpec as P

BF16 = jnp.bfloat16
F32 = jnp.float32
I32 = jnp.int32
HIGHEST = lax.Precision.HIGHEST
VMEM_BYTES = 32 * 1024 * 1024


def dot_nn(a, b, precision=None):
    return lax.dot_general(
        a, b, (((1,), (0,)), ((), ())), precision=precision, preferred_element_type=F32
    )


def dot_nt(a, b, precision=None):
    return lax.dot_general(
        a, b, (((1,), (1,)), ((), ())), precision=precision, preferred_element_type=F32
    )


def iota(shape, dim):
    return lax.broadcasted_iota(I32, shape, dim)


def floor_div(values, by):
    return jnp.floor((values.astype(F32) + 0.5) * (1.0 / by)).astype(I32)


def whole(memory_space=pltpu.VMEM):
    return pl.BlockSpec(memory_space=memory_space)


def tail_rows(block, chunks):
    return -(-(block * chunks) // 16) * 16


def masked_rows(panel, count):
    live = iota(panel.shape, 0) < count
    return jnp.where(live, panel.astype(F32), 0.0).astype(BF16)


def pack_kernel(block, width, chunks, panels, amps, count, out, held, sem):
    first = lax.axis_index("aux") * block
    copy = pltpu.make_async_copy(panels.at[pl.ds(first, block)], held, sem)
    copy.start()
    pao = held.shape[2]
    pairs = amps.shape[0]
    tail = tail_rows(block, chunks)
    row = iota((tail, pairs), 0)
    source = iota((tail, pairs), 1)
    rows = jnp.zeros((tail, pao), F32)
    for chunk in range(chunks):
        inside = (row >= chunk * block) & (row < (chunk + 1) * block)
        hot = (inside & (source == first + row - chunk * block)).astype(F32).astype(BF16)
        rows += dot_nn(hot, amps[:, chunk * pao : (chunk + 1) * pao])
    out[block * width :, :] = rows.astype(BF16)
    copy.wait()
    for j in range(block):
        out[j * width : (j + 1) * width, :] = masked_rows(held[j], count[first + j])


def pack(panels, amps, count, block):
    pairs, width, pao = panels.shape
    chunks = width * width // pao
    rows = block * width + tail_rows(block, chunks)
    return pl.pallas_call(
        functools.partial(pack_kernel, block, width, chunks),
        out_shape=jax.ShapeDtypeStruct((rows, pao), BF16),
        in_specs=[whole(pl.ANY), whole(), whole(pltpu.SMEM)],
        out_specs=whole(),
        scratch_shapes=[pltpu.VMEM((block, width, pao), BF16), pltpu.SemaphoreType.DMA],
        compiler_params=pltpu.CompilerParams(vmem_limit_bytes=VMEM_BYTES),
        name="pack",
    )(panels, amps, count)


def exchange_kernel(group, width, fit, panels, count, out, masked):
    step = pl.program_id(0)
    functions = fit.shape[2]
    for g in range(group):
        panel = masked_rows(panels[g], count[step * group + g])
        masked[g * width : (g + 1) * width, :] = panel
        if functions % 128 == 0:
            both = dot_nt(panel, fit[g].reshape(2 * functions, fit.shape[3])).astype(BF16)
            left, right = both[:, :functions], both[:, functions:]
        else:
            left = dot_nt(panel, fit[g, 0]).astype(BF16)
            right = dot_nt(panel, fit[g, 1]).astype(BF16)
        out[g * width : (g + 1) * width, :] = dot_nt(left, right)


def exchange(fit, panels, count):
    pairs, width, pao = panels.shape
    functions = fit.shape[2]
    group = 4
    flops = 2 * pairs * (2 * functions * pao * width + functions * width * width)
    return pl.pallas_call(
        functools.partial(exchange_kernel, group, width),
        out_shape=(
            jax.ShapeDtypeStruct((pairs * width, width), F32),
            jax.ShapeDtypeStruct((pairs * width, pao), BF16),
        ),
        grid=(pairs // group,),
        in_specs=[
            pl.BlockSpec((group, 2, functions, pao), lambda i: (i, 0, 0, 0)),
            pl.BlockSpec((group, width, pao), lambda i: (i, 0, 0)),
            whole(pltpu.SMEM),
        ],
        out_specs=(
            pl.BlockSpec((group * width, width), lambda i: (i, 0)),
            pl.BlockSpec((group * width, pao), lambda i: (i, 0)),
        ),
        compiler_params=pltpu.CompilerParams(vmem_limit_bytes=VMEM_BYTES),
        cost_estimate=pl.CostEstimate(
            flops=5 * flops, bytes_accessed=fit.size * 2 + panels.size * 4, transcendentals=0
        ),
        name="exchange",
    )(fit, panels, count)


def tables_kernel(
    block, width, couplings, rounds, table, pos, fock, amps, weight_in, weight_out, block_amps
):
    total = pos.shape[0]
    occ = fock.shape[0]
    per_dev = amps.shape[0] // width
    rows = table.shape[0]
    pair_devices = total // per_dev
    pair = lax.axis_index("pair")
    first = lax.axis_index("aux") * block
    here = pos[...] == iota((total, total), 1)
    label_at = jnp.sum(jnp.where(here, iota((total, total), 0), 0), axis=0, keepdims=True)
    lanes = iota((rows, occ), 1)
    base = 3 * couplings
    hot_i = (table[:, base : base + 1] == lanes).astype(F32)
    hot_j = (table[:, base + 1 : base + 2] == lanes).astype(F32)
    fock_i = dot_nn(hot_i, fock[...], HIGHEST)
    fock_j = dot_nt(hot_j, fock[...], HIGHEST)
    weight = jnp.zeros((rows, total), F32)
    for c in range(couplings):
        hot_k = table[:, 2 * couplings + c : 2 * couplings + c + 1] == lanes
        left = jnp.sum(jnp.where(hot_k, fock_j, 0.0), axis=1, keepdims=True)
        right = jnp.sum(jnp.where(hot_k, fock_i, 0.0), axis=1, keepdims=True)
        weight += jnp.where(table[:, 2 * c : 2 * c + 1] == label_at, left, 0.0)
        weight += jnp.where(table[:, 2 * c + 1 : 2 * c + 2] == label_at, right, 0.0)
    wide = per_dev * width
    spread = (
        iota((total, wide), 0) == pair * per_dev + floor_div(iota((total, wide), 1), width)
    ).astype(F32)
    weight_out[...] = dot_nn(weight[per_dev:, :], spread, HIGHEST)
    thin = block * width
    of_row = iota((total, thin), 0)
    of_lane = floor_div(iota((total, thin), 1), width)
    for k in range(rounds + 1):
        source = lax.rem(pair + pair_devices - k, pair_devices) * per_dev + first
        spread = (of_row == source + of_lane).astype(F32)
        weight_in[k * per_dev : (k + 1) * per_dev, :] = dot_nn(
            weight[:per_dev, :], spread, HIGHEST
        )
    lane = iota((1, wide), 1)
    lane_pair = floor_div(lane, width)
    repeat = (iota((width, wide), 0) == (lane - width * lane_pair)).astype(F32).astype(BF16)
    tiled = dot_nn(amps[...], repeat)
    row_pair = floor_div(iota((wide, 1), 0), width)
    block_amps[...] = jnp.where(row_pair == lane_pair, tiled, 0.0).astype(BF16)


def tables(table, pos, fock, amps, block, width, couplings, rounds):
    wide = amps.shape[0]
    per_dev = wide // width
    return pl.pallas_call(
        functools.partial(tables_kernel, block, width, couplings, rounds),
        out_shape=(
            jax.ShapeDtypeStruct(((rounds + 1) * per_dev, block * width), F32),
            jax.ShapeDtypeStruct((table.shape[0] - per_dev, wide), F32),
            jax.ShapeDtypeStruct((wide, wide), BF16),
        ),
        in_specs=[whole()] * 4,
        out_specs=(whole(),) * 3,
        compiler_params=pltpu.CompilerParams(vmem_limit_bytes=VMEM_BYTES),
        cost_estimate=pl.CostEstimate(
            flops=2_000_000_000, bytes_accessed=4_000_000, transcendentals=0
        ),
        name="tables",
    )(table, pos, fock, amps)


def split_high_low(values):
    high = values.astype(BF16)
    return high, (values - high.astype(F32)).astype(BF16)


def couple_kernel(block, width, chunks, back, flat, *refs):
    refs = list(refs)
    sent, masked, weight_in, acc_in = refs[:4]
    refs = refs[4:]
    if back:
        block_amps, weight_out = refs[:2]
        refs = refs[2:]
    acc_out = refs.pop(0)
    if back:
        back_out = refs.pop(0)
    acc = refs.pop(0) if flat else acc_out
    if back:
        back_acc = refs.pop(0)
    thin = block * width
    pao = masked.shape[1]
    per_dev = masked.shape[0] // width
    per_chunk = pao // width
    tail = sent.shape[0] - thin
    panels = sent[:thin, :]

    row = iota((thin, 1), 0)
    row_pair = floor_div(row, width)
    row_pno = row - width * row_pair
    row_chunk = floor_div(row_pno, per_chunk)
    pick = (iota((thin, tail), 1) == row_chunk * block + row_pair).astype(F32).astype(BF16)
    picked = dot_nn(pick, sent[thin:, :])
    lane = iota((1, pao), 1)
    picked = jnp.where(
        row_pno - per_chunk * row_chunk == floor_div(lane, width), picked, 0.0
    ).astype(BF16)
    down = iota((pao, 1), 0)
    across = iota((1, thin), 1)
    across_pair = floor_div(across, width)
    fold = (
        (down - width * floor_div(down, width)) == (across - width * across_pair)
    ).astype(F32).astype(BF16)
    sent_amps = jnp.where(row_pair == across_pair, dot_nn(picked, fold), 0.0).astype(BF16)

    inter = dot_nt(masked[...], panels).astype(BF16)
    half = dot_nn(inter, sent_amps).astype(BF16).astype(F32)
    for t in range(per_dev):
        rows = slice(t * width, (t + 1) * width)
        high, low = split_high_low(half[rows, :] * weight_in[t : t + 1, :])
        mine = inter[rows, :]
        acc[rows, :] = acc_in[rows, :] - (dot_nt(high, mine) + dot_nt(low, mine))
    if flat:
        for a in range(width):
            acc_out[:, a * width : (a + 1) * width] = acc[pl.ds(a, per_dev, stride=width), :]
    if back:
        inter = dot_nt(panels, masked[...]).astype(BF16)
        half = dot_nn(inter, block_amps[...]).astype(BF16).astype(F32)
        for s in range(block):
            rows = slice(s * width, (s + 1) * width)
            high, low = split_high_low(half[rows, :] * weight_out[s : s + 1, :])
            mine = inter[rows, :]
            back_acc[rows, :] = dot_nt(high, mine) + dot_nt(low, mine)
        for a in range(width):
            back_out[:, a * width : (a + 1) * width] = back_acc[pl.ds(a, block, stride=width), :]


def couple(sent, masked, weight_in, acc, block, width, flat, back):
    pao = masked.shape[1]
    wide = masked.shape[0]
    per_dev = wide // width
    chunks = width * width // pao
    thin = block * width
    acc_shape = (per_dev, width * width) if flat else (wide, width)
    outs = [jax.ShapeDtypeStruct(acc_shape, F32)]
    scratch = [pltpu.VMEM((wide, width), F32)] if flat else []
    if back:
        outs.append(jax.ShapeDtypeStruct((block, width * width), F32))
        scratch.append(pltpu.VMEM((thin, width), F32))
    args = (sent, masked, weight_in, acc) + tuple(back or ())
    flops = 2 * thin * wide * (pao + thin) + (2 * thin * wide * (pao + wide) if back else 0)
    return pl.pallas_call(
        functools.partial(couple_kernel, block, width, chunks, bool(back), flat),
        out_shape=tuple(outs),
        in_specs=[whole()] * len(args),
        out_specs=(whole(),) * len(outs),
        scratch_shapes=scratch,
        compiler_params=pltpu.CompilerParams(vmem_limit_bytes=VMEM_BYTES),
        cost_estimate=pl.CostEstimate(flops=flops, bytes_accessed=3_000_000, transcendentals=0),
        name="couple",
    )(*args)


def senders(devices, k):
    if 2 * k != devices:
        return list(range(devices))
    return [p for p in range(devices) if (p < k) == (p % 2 == 0)]


def on_device(
    panels,
    amplitudes,
    fitted_ints,
    pno_energy,
    fock_occ,
    pno_count,
    pair_pos,
    coupling,
    coupling_lmo,
    pair_lmo,
):
    per_dev, width, pao = panels.shape
    pair_devices = lax.axis_size("pair")
    aux_devices = lax.axis_size("aux")
    block = per_dev // aux_devices
    couplings = coupling.shape[1]
    total = pair_pos.shape[0]
    rounds = pair_devices // 2
    pair = lax.axis_index("pair")
    aux = lax.axis_index("aux")

    sent = pack(panels, amplitudes, pno_count, block)
    arrived = []
    for k in range(1, rounds + 1):
        ways = [(p, (p + k) % pair_devices) for p in senders(pair_devices, k)]
        arrived.append((ways, lax.ppermute(sent, "pair", ways)))

    acc, masked = exchange(fitted_ints, panels, pno_count)

    table = jnp.concatenate([coupling.reshape(total, 2 * couplings), coupling_lmo, pair_lmo], 1)
    table = jnp.pad(table, ((0, 0), (0, 128 - table.shape[1])))
    pieces = [lax.dynamic_slice_in_dim(table, pair * per_dev, per_dev, 0)]
    for k in range(1, rounds + 1):
        source = lax.rem(pair + pair_devices - k, pair_devices) * per_dev + aux * block
        piece = lax.dynamic_slice_in_dim(table, source, block, 0)
        pieces.append(jnp.pad(piece, ((0, 8 - block), (0, 0))))
    weight_in, weight_out, block_amps = tables(
        jnp.concatenate(pieces, 0),
        pair_pos[:, None],
        fock_occ,
        amplitudes.reshape(per_dev * width, width),
        block,
        width,
        couplings,
        rounds,
    )

    own_first = aux * block
    live = iota((block, width), 1) < lax.dynamic_slice_in_dim(pno_count, own_first, block)[:, None]
    live = live[:, :, None] & live[:, None, :]
    own_energy = lax.dynamic_slice_in_dim(pno_energy, own_first, block, 0)
    own_lmo = lax.dynamic_slice_in_dim(pair_lmo, pair * per_dev + own_first, block, 0)
    occ_diag = jnp.diagonal(fock_occ)
    lmo_hot = own_lmo[:, :, None] == jnp.arange(fock_occ.shape[0], dtype=I32)
    occ_pair = jnp.sum(jnp.where(lmo_hot, occ_diag, 0.0), axis=(1, 2))
    gap = own_energy[:, :, None] + own_energy[:, None, :] - occ_pair[:, None, None]
    gap = jnp.where(live, gap, 0.0).reshape(block, width * width)
    own_amps = lax.dynamic_slice_in_dim(amplitudes, own_first, block, 0)
    own = gap * own_amps.astype(F32)

    (acc,) = couple(sent, masked, weight_in[:per_dev], acc, block, width, False, None)
    for k, (ways, block_sent) in enumerate(arrived, 1):
        acc, back = couple(
            block_sent,
            masked,
            weight_in[k * per_dev : (k + 1) * per_dev],
            acc,
            block,
            width,
            k == rounds,
            (block_amps, weight_out[(k - 1) * 8 : k * 8]),
        )
        own = own - lax.ppermute(back, "pair", [(q, p) for p, q in ways])

    left = acc.reshape(aux_devices, block, width * width)
    step = 1
    while step < aux_devices:
        bit = (aux // step) % 2
        halves = left.reshape(left.shape[0] // 2, 2, block, width * width)
        keep = lax.dynamic_index_in_dim(halves, bit, 1, False)
        give = lax.dynamic_index_in_dim(halves, 1 - bit, 1, False)
        ways = [(d, d ^ step) for d in range(aux_devices)]
        left = keep + lax.ppermute(give, "aux", ways)
        step *= 2
    return left[0] + own


def solution(mesh):
    placed = (
        P(("groups", "pair"), None, None),
        P(("groups", "pair"), None),
        P(("groups", "pair"), None, "aux", None),
        P(("groups", "pair"), None),
        P("groups", None),
        P(("groups", "pair")),
        P("groups"),
        P("groups", None, None),
        P("groups", None),
        P("groups", None),
    )
    return jax.shard_map(
        on_device,
        mesh=mesh,
        in_specs=placed,
        out_specs=P(("groups", "pair", "aux"), None),
        check_vma=False,
    )
```

```python
import functools

import jax
import jax.numpy as jnp
from jax import lax
from jax.experimental import pallas as pl
from jax.experimental.pallas import tpu as pltpu
from jax.sharding import PartitionSpec as P

BF16 = jnp.bfloat16
F32 = jnp.float32
I32 = jnp.int32
HIGHEST = lax.Precision.HIGHEST
VMEM_BYTES = 48 * 1024 * 1024
PACK_VMEM_BYTES = 61 * 1024 * 1024
LOCAL_VMEM_BYTES = 48 * 1024 * 1024


def dot_nn(a, b, precision=None):
    return lax.dot_general(
        a, b, (((1,), (0,)), ((), ())), precision=precision, preferred_element_type=F32
    )


def dot_nt(a, b, precision=None):
    return lax.dot_general(
        a, b, (((1,), (1,)), ((), ())), precision=precision, preferred_element_type=F32
    )


def iota(shape, dim):
    return lax.broadcasted_iota(I32, shape, dim)


def floor_div(values, by):
    return jnp.floor((values.astype(F32) + 0.5) * (1.0 / by)).astype(I32)


def whole(memory_space=pltpu.VMEM):
    return pl.BlockSpec(memory_space=memory_space)


def lane_in(width, lanes):
    lane = iota((1, lanes), 1)
    block = floor_div(lane, width)
    return block, lane - width * block


def row_in(width, rows):
    row = iota((rows, 1), 0)
    block = floor_div(row, width)
    return block, row - width * block


def fold_diagonal(square, width):
    lanes = square.shape[1]
    block, _ = lane_in(width, lanes)
    out = jnp.zeros((width, lanes), F32)
    for n in range(lanes // width):
        out += jnp.where(block == n, square[n * width : (n + 1) * width, :], 0.0)
    return out


def tail_rows(block, chunks):
    return -(-(block * chunks) // 16) * 16


def masked_rows(panel, count):
    live = iota(panel.shape, 0) < count
    return jnp.where(live, panel.astype(F32), 0.0).astype(BF16)


def split_high_low(values):
    high = values.astype(BF16)
    return high, (values - high.astype(F32)).astype(BF16)


def pack_kernel(block, width, chunks, panels, amps, count, out, held, amps_held, count_held, sems):
    first = lax.axis_index("aux") * block
    copies = [
        pltpu.make_async_copy(panels.at[pl.ds(first, block)], held, sems.at[0]),
        pltpu.make_async_copy(amps, amps_held, sems.at[1]),
        pltpu.make_async_copy(count, count_held, sems.at[2]),
    ]
    for copy in copies:
        copy.start()
    pao = held.shape[2]
    pairs = amps_held.shape[0]
    tail = tail_rows(block, chunks)
    row = iota((tail, pairs), 0)
    source = iota((tail, pairs), 1)
    for copy in copies:
        copy.wait()
    rows = jnp.zeros((tail, pao), F32)
    for chunk in range(chunks):
        inside = (row >= chunk * block) & (row < (chunk + 1) * block)
        hot = (inside & (source == first + row - chunk * block)).astype(F32).astype(BF16)
        rows += dot_nn(hot, amps_held[:, chunk * pao : (chunk + 1) * pao])
    out[block * width :, :] = rows.astype(BF16)
    for j in range(block):
        out[j * width : (j + 1) * width, :] = masked_rows(held[j], count_held[first + j])


def pack(panels, amps, count, block):
    pairs, width, pao = panels.shape
    chunks = width * width // pao
    rows = block * width + tail_rows(block, chunks)
    return pl.pallas_call(
        functools.partial(pack_kernel, block, width, chunks),
        out_shape=jax.ShapeDtypeStruct((rows, pao), BF16),
        in_specs=[whole(pltpu.HBM)] * 3,
        out_specs=whole(),
        scratch_shapes=[
            pltpu.VMEM((block, width, pao), BF16),
            pltpu.VMEM(amps.shape, BF16),
            pltpu.SMEM(count.shape, I32),
            pltpu.SemaphoreType.DMA((3,)),
        ],
        compiler_params=pltpu.CompilerParams(vmem_limit_bytes=PACK_VMEM_BYTES),
        name="pack",
    )(panels, amps, count)


def local_kernel(
    block,
    width,
    ways,
    coupling,
    orbital,
    lmo,
    pos,
    fock,
    amps,
    energy,
    count,
    fit,
    panels,
    weight_in,
    weight_out,
    block_amps,
    own,
    masked,
    out,
    weight,
    fock_of,
    held,
    panels_held,
    count_held,
    both,
    sems,
):
    copies = [
        pltpu.make_async_copy(count, count_held, sems.at[0]),
        pltpu.make_async_copy(panels, panels_held, sems.at[1]),
    ]
    groups = fit.shape[0] // block
    fits = []
    for group in range(groups):
        part = pl.ds(group * block, block)
        fits.append(pltpu.make_async_copy(fit.at[part], held.at[part], sems.at[2 + group]))
    for copy in copies + fits:
        copy.start()
    total = pos.shape[1]
    occ = fock.shape[0]
    couplings = orbital.shape[0]
    per_dev = energy.shape[0]
    pair_devices = total // per_dev
    pair = lax.axis_index("pair")
    first = lax.axis_index("aux") * block
    here = pos[...] == iota((total, total), 0)
    label_at = jnp.sum(jnp.where(here, iota((total, total), 1), 0), axis=1, keepdims=True)
    level = iota((occ, total), 0)
    hot_i = (lmo[0:1, :] == level).astype(F32)
    hot_j = (lmo[1:2, :] == level).astype(F32)
    fock_of[0] = dot_nn(fock[...], hot_j, HIGHEST)
    fock_of[1] = lax.dot_general(
        fock[...], hot_i, (((0,), (0,)), ((), ())), precision=HIGHEST, preferred_element_type=F32
    )
    weight[...] = jnp.zeros_like(weight)

    def add(c, carry):
        hot_k = orbital[pl.ds(c, 1), :] == level
        for h in range(2):
            value = jnp.sum(jnp.where(hot_k, fock_of[h], 0.0), axis=0, keepdims=True)
            named = coupling[pl.ds(2 * c + h, 1), :] == label_at
            weight[...] += jnp.where(named, value, 0.0)
        return carry

    lax.fori_loop(0, couplings, add, 0, unroll=4)

    def of_pairs(rows, start):
        hot = (iota((rows, total), 1) == start + iota((rows, total), 0)).astype(F32)
        return dot_nt(hot, weight[...], HIGHEST)

    wide = per_dev * width
    thin = block * width
    wide_pair, wide_pno = lane_in(width, wide)
    thin_pair, _ = lane_in(width, thin)
    mine = of_pairs(per_dev, pair * per_dev)
    local = (iota((total, wide), 0) == pair * per_dev + wide_pair).astype(F32)
    for k in range(len(ways) + 1):
        start = pair
        if k > 0:
            start = jnp.int32(-pair_devices)
            for sender, receiver in ways[k - 1]:
                start = jnp.where(pair == receiver, sender, start)
        source = start * per_dev + first
        spread = (iota((total, thin), 0) == source + thin_pair).astype(F32)
        weight_in[k] = dot_nn(mine, spread, HIGHEST)
        if k > 0:
            weight_out[k - 1] = dot_nn(of_pairs(8, source), local, HIGHEST)

    repeat = (iota((width, wide), 0) == wide_pno).astype(F32).astype(BF16)
    tiled = dot_nn(amps[...], repeat)
    row_pair, _ = row_in(width, wide)
    block_amps[...] = jnp.where(row_pair == wide_pair, tiled, 0.0).astype(BF16)

    for copy in copies:
        copy.wait()
    across = iota((occ, occ), 0) == iota((occ, occ), 1)
    diagonal = jnp.sum(jnp.where(across, fock[...], 0.0), axis=1, keepdims=True)
    gap_of = jnp.sum((hot_i + hot_j) * diagonal, axis=0, keepdims=True)
    row = iota((width, width), 0)
    column = iota((width, width), 1)
    for j in range(block):
        at = iota((1, total), 1) == pair * per_dev + first + j
        gap = jnp.sum(jnp.where(at, gap_of, 0.0), axis=1, keepdims=True)
        flat = energy[pl.ds(first + j, 1), :]
        upright = jnp.sum(jnp.where(row == column, flat, 0.0), axis=1, keepdims=True)
        live = count_held[first + j]
        values = amps[pl.ds((first + j) * width, width), :].astype(F32)
        term = (upright + flat - gap) * values
        own[:, j * width : (j + 1) * width] = jnp.where((row < live) & (column < live), term, 0.0)

    functions = held.shape[2]
    pao = held.shape[3]
    for p in range(per_dev):
        masked[p * width : (p + 1) * width, :] = masked_rows(panels_held[p], count_held[p])
    for group in range(groups):
        fits[group].wait()
        for p in range(group * block, (group + 1) * block):
            rows = slice(p * width, (p + 1) * width)
            if functions % 128 == 0:
                fitted = dot_nt(masked[rows, :], held[p].reshape(2 * functions, pao)).astype(BF16)
                both[0, rows, :] = fitted[:, :functions]
                both[1, rows, :] = fitted[:, functions:]
            else:
                for h in range(2):
                    both[h, rows, :] = dot_nt(masked[rows, :], held[p, h]).astype(BF16)
        rows = slice(group * thin, (group + 1) * thin)
        out[group] = fold_diagonal(dot_nt(both[0, rows, :], both[1, rows, :]), width)


def local(coupling, orbital, lmo, pos, fock, amps, energy, count, fit, panels, block, ways):
    rounds = len(ways)
    wide, width = amps.shape
    per_dev, _, pao = panels.shape
    total = pos.shape[1]
    occ = fock.shape[0]
    groups = per_dev // block
    thin = block * width
    return pl.pallas_call(
        functools.partial(local_kernel, block, width, ways),
        out_shape=(
            jax.ShapeDtypeStruct((rounds + 1, per_dev, thin), F32),
            jax.ShapeDtypeStruct((rounds, 8, wide), F32),
            jax.ShapeDtypeStruct((wide, wide), BF16),
            jax.ShapeDtypeStruct((width, thin), F32),
            jax.ShapeDtypeStruct((wide, pao), BF16),
            jax.ShapeDtypeStruct((groups, width, thin), F32),
        ),
        in_specs=[whole()] * 7 + [whole(pltpu.HBM)] * 3,
        out_specs=(whole(),) * 6,
        scratch_shapes=[
            pltpu.VMEM((total, total), F32),
            pltpu.VMEM((2, occ, total), F32),
            pltpu.VMEM(fit.shape, BF16),
            pltpu.VMEM(panels.shape, BF16),
            pltpu.SMEM(count.shape, I32),
            pltpu.VMEM((2, wide, fit.shape[2]), BF16),
            pltpu.SemaphoreType.DMA((2 + groups,)),
        ],
        compiler_params=pltpu.CompilerParams(vmem_limit_bytes=LOCAL_VMEM_BYTES),
        cost_estimate=pl.CostEstimate(
            flops=6_000_000_000, bytes_accessed=fit.size * 2, transcendentals=0
        ),
        name="local",
    )(coupling, orbital, lmo, pos, fock, amps, energy, count, fit, panels)


def unpack_amps(sent, block, width):
    thin = block * width
    pao = sent.shape[1]
    per_chunk = pao // width
    row_pair, row_pno = row_in(width, thin)
    row_chunk = floor_div(row_pno, per_chunk)
    tail = sent.shape[0] - thin
    pick = (iota((thin, tail), 1) == row_chunk * block + row_pair).astype(F32).astype(BF16)
    picked = dot_nn(pick, sent[thin:, :])
    lane_block, _ = lane_in(width, pao)
    at = row_pno - per_chunk * row_chunk == lane_block
    picked = jnp.where(at, picked, 0.0).astype(BF16)
    _, down_pno = row_in(width, pao)
    across_pair, across_pno = lane_in(width, thin)
    fold = (down_pno == across_pno).astype(F32).astype(BF16)
    return jnp.where(row_pair == across_pair, dot_nn(picked, fold), 0.0).astype(BF16)


def add_in(block, width, masked, parts, put):
    thin = block * width
    inters, halves = [], []
    for sent, _ in parts:
        inter = dot_nt(masked[...], sent[:thin, :]).astype(BF16)
        half = dot_nn(inter, unpack_amps(sent, block, width)).astype(BF16).astype(F32)
        inters.append(inter)
        halves.append(half)
    for group in range(masked.shape[0] // thin):
        square = jnp.zeros((thin, thin), F32)
        for (_, weight_in), inter, half in zip(parts, inters, halves):
            scaled = []
            for t in range(group * block, (group + 1) * block):
                scaled.append(half[t * width : (t + 1) * width, :] * weight_in[t : t + 1, :])
            high, low = split_high_low(jnp.concatenate(scaled, 0))
            mine = inter[group * thin : (group + 1) * thin, :]
            square += dot_nt(high, mine) + dot_nt(low, mine)
        put(group, fold_diagonal(square, width))


def add_back(block, width, sent, masked, block_amps, weight_out):
    thin = block * width
    inter = dot_nt(sent[:thin, :], masked[...]).astype(BF16)
    half = dot_nn(inter, block_amps[...]).astype(BF16).astype(F32)
    parts = []
    for s in range(block):
        parts.append(half[s * width : (s + 1) * width, :] * weight_out[s : s + 1, :])
    high, low = split_high_low(jnp.concatenate(parts, 0))
    return fold_diagonal(dot_nt(high, inter) + dot_nt(low, inter), width)


def back_kernel(block, width, sent, masked, block_amps, weight_out, out):
    out[...] = as_sent(add_back(block, width, sent, masked, block_amps, weight_out)).astype(BF16)


def both_kernel(block, width, *refs):
    masked, block_amps, acc, sent, weight_in, weight_out = refs[:6]
    out, back = refs[-2:]
    parts = [(sent, weight_in)] + ([refs[6:8]] if len(refs) > 8 else [])

    def put(group, value):
        out[group] = acc[group] - value

    back[...] = as_sent(add_back(block, width, sent, masked, block_amps, weight_out)).astype(BF16)
    add_in(block, width, masked, parts, put)


def last_kernel(block, width, returned, sent, masked, weight_in, acc, own, *refs):
    backs, outs, held = refs[:returned], refs[returned:-1], refs[-1]

    def put(group, value):
        held[group] = acc[group] - value

    add_in(block, width, masked, [(sent, weight_in)], put)
    aux = lax.axis_index("aux")
    mine = as_sent(held[aux] + own[...])
    for back in backs:
        mine -= back[...].astype(F32)
    outs[0][...] = mine
    for k in range(1, len(outs)):
        outs[k][...] = as_sent(held[lax.bitwise_xor(aux, k)]).astype(BF16)


def finish_kernel(block, width, count, *refs):
    parts, out, held = refs[:count], refs[count], refs[count + 1]
    total = parts[0][...]
    for part in parts[1:-1]:
        total += part[...].astype(F32)
    total -= parts[-1][...].astype(F32)
    for s in range(block):
        for r in range(0, width, 16):
            lane = r // 16 * block * width + s * width
            held[s * width + r : s * width + r + 16, :] = total[:, lane : lane + width]
    for a in range(width):
        out[:, a * width : (a + 1) * width] = held[pl.ds(a, block, stride=width), :]


def as_sent(values):
    rows = values.shape[0]
    return jnp.concatenate([values[r : r + 16, :] for r in range(0, rows, 16)], 1)


def call(kernel, name, out_shape, args, flops, scratch=()):
    many = isinstance(out_shape, tuple)
    return pl.pallas_call(
        kernel,
        out_shape=out_shape,
        in_specs=[whole()] * len(args),
        out_specs=(whole(),) * len(out_shape) if many else whole(),
        scratch_shapes=list(scratch),
        compiler_params=pltpu.CompilerParams(vmem_limit_bytes=VMEM_BYTES),
        cost_estimate=pl.CostEstimate(flops=flops, bytes_accessed=3_000_000, transcendentals=0),
        name=name,
    )(*args)


def schedule(devices):
    if devices == 4:
        return [[(0, 2), (3, 1), (2, 3), (1, 0)], [(1, 2), (3, 0)]]
    rounds = []
    for k in range(1, devices // 2 + 1):
        whole_way = [(p, (p + k) % devices) for p in range(devices)]
        if 2 * k == devices:
            whole_way = [way for way in whole_way if (way[0] < k) == (way[0] % 2 == 0)]
        rounds.append(whole_way)
    return rounds


def completed(way, devices):
    idle = sorted(set(range(devices)) - {p for p, _ in way})
    open_ends = sorted(set(range(devices)) - {q for _, q in way})
    return way + list(zip(idle, open_ends))


def on_device(
    panels,
    amplitudes,
    fitted_ints,
    pno_energy,
    fock_occ,
    pno_count,
    pair_pos,
    coupling,
    coupling_lmo,
    pair_lmo,
):
    per_dev, width, pao = panels.shape
    pair_devices = lax.axis_size("pair")
    aux_devices = lax.axis_size("aux")
    block = per_dev // aux_devices
    thin = block * width
    couplings = coupling.shape[1]
    total = pair_pos.shape[0]
    ways = schedule(pair_devices)
    rounds = len(ways)
    back_ways = [completed([(q, p) for p, q in way], pair_devices) for way in ways]

    sent = pack(panels, amplitudes, pno_count, block)
    arrived = [lax.ppermute(sent, "pair", way) for way in ways]
    weight_in, weight_out, block_amps, own, masked, acc = local(
        coupling.transpose(1, 2, 0).reshape(2 * couplings, total),
        coupling_lmo.T,
        pair_lmo.T,
        pair_pos[None, :],
        fock_occ,
        amplitudes.reshape(per_dev * width, width),
        pno_energy,
        pno_count,
        fitted_ints,
        panels,
        block,
        ways,
    )

    acc_shape = jax.ShapeDtypeStruct(acc.shape, F32)
    own_shape = jax.ShapeDtypeStruct((16, width // 16 * thin), F32)
    block_shape = jax.ShapeDtypeStruct(own_shape.shape, BF16)
    flops = 1_000_000_000
    returned = []
    for k in range(1, rounds):
        args = (masked, block_amps, acc, arrived[k - 1], weight_in[k], weight_out[k - 1])
        if k == 1:
            args += (sent, weight_in[0])
        acc, back = call(
            functools.partial(both_kernel, block, width),
            "couple",
            (acc_shape, block_shape),
            args,
            2 * flops,
        )
        returned.append(lax.ppermute(back, "pair", back_ways[k - 1]))
    back = call(
        functools.partial(back_kernel, block, width),
        "couple_back",
        block_shape,
        (arrived[-1], masked, block_amps, weight_out[-1]),
        flops,
    )
    last_back = lax.ppermute(back, "pair", back_ways[-1])
    parts = call(
        functools.partial(last_kernel, block, width, len(returned)),
        "couple_last",
        (own_shape,) + (block_shape,) * (aux_devices - 1),
        (arrived[-1], masked, weight_in[rounds], acc, own, *returned),
        flops,
        [pltpu.VMEM(acc.shape, F32)],
    )
    sums = [parts[0]]
    for k in range(1, aux_devices):
        sums.append(lax.ppermute(parts[k], "aux", [(d, d ^ k) for d in range(aux_devices)]))
    sums.append(last_back)
    return call(
        functools.partial(finish_kernel, block, width, len(sums)),
        "finish",
        jax.ShapeDtypeStruct((block, width * width), F32),
        tuple(sums),
        1_000_000,
        [pltpu.VMEM((thin, width), F32)],
    )


def solution(mesh):
    placed = (
        P(("groups", "pair"), None, None),
        P(("groups", "pair"), None),
        P(("groups", "pair"), None, "aux", None),
        P(("groups", "pair"), None),
        P("groups", None),
        P(("groups", "pair")),
        P("groups"),
        P("groups", None, None),
        P("groups", None),
        P("groups", None),
    )
    return jax.shard_map(
        on_device,
        mesh=mesh,
        in_specs=placed,
        out_specs=P(("groups", "pair", "aux"), None),
        check_vma=False,
    )
```

```python
import functools

import jax
import jax.numpy as jnp
from jax import lax
from jax.experimental import pallas as pl
from jax.experimental.pallas import tpu as pltpu
from jax.sharding import PartitionSpec as P

BF16 = jnp.bfloat16
F32 = jnp.float32
I32 = jnp.int32
HIGHEST = lax.Precision.HIGHEST
VMEM_BYTES = 48 * 1024 * 1024
PACK_VMEM_BYTES = 61 * 1024 * 1024
LOCAL_VMEM_BYTES = 48 * 1024 * 1024


def dot_nn(a, b, precision=None):
    return lax.dot_general(
        a, b, (((1,), (0,)), ((), ())), precision=precision, preferred_element_type=F32
    )


def dot_nt(a, b, precision=None):
    return lax.dot_general(
        a, b, (((1,), (1,)), ((), ())), precision=precision, preferred_element_type=F32
    )


def iota(shape, dim):
    return lax.broadcasted_iota(I32, shape, dim)


def floor_div(values, by):
    return jnp.floor((values.astype(F32) + 0.5) * (1.0 / by)).astype(I32)


def whole(memory_space=pltpu.VMEM):
    return pl.BlockSpec(memory_space=memory_space)


def lane_in(width, lanes):
    lane = iota((1, lanes), 1)
    block = floor_div(lane, width)
    return block, lane - width * block


def row_in(width, rows):
    row = iota((rows, 1), 0)
    block = floor_div(row, width)
    return block, row - width * block


def fold_diagonal(square, width):
    lanes = square.shape[1]
    block, _ = lane_in(width, lanes)
    out = jnp.zeros((width, lanes), F32)
    for n in range(lanes // width):
        out += jnp.where(block == n, square[n * width : (n + 1) * width, :], 0.0)
    return out


def tail_rows(block, chunks):
    return -(-(block * chunks) // 16) * 16


def masked_rows(panel, count):
    live = iota(panel.shape, 0) < count
    return jnp.where(live, panel.astype(F32), 0.0).astype(BF16)


def split_high_low(values):
    high = values.astype(BF16)
    return high, (values - high.astype(F32)).astype(BF16)


def pack_kernel(block, width, chunks, panels, amps, count, out, held, amps_held, count_held, made, sems):
    first = lax.axis_index("aux") * block
    coming = [
        pltpu.make_async_copy(amps, amps_held, sems.at[0]),
        pltpu.make_async_copy(count, count_held, sems.at[1]),
    ]
    for j in range(block):
        coming.append(pltpu.make_async_copy(panels.at[first + j], held.at[j], sems.at[2 + j]))
    for copy in coming:
        copy.start()
    pao = held.shape[2]
    pairs = amps_held.shape[0]
    tail = tail_rows(block, chunks)
    row = iota((tail, pairs), 0)
    source = iota((tail, pairs), 1)
    hots = []
    for chunk in range(chunks):
        inside = (row >= chunk * block) & (row < (chunk + 1) * block)
        hots.append((inside & (source == first + row - chunk * block)).astype(F32).astype(BF16))
    going = []

    def send(start, rows):
        part = pl.ds(start, rows)
        sem = sems.at[2 + block + len(going)]
        going.append(pltpu.make_async_copy(made.at[part], out.at[part], sem))
        going[-1].start()

    coming[0].wait()
    rows = jnp.zeros((tail, pao), F32)
    for chunk, hot in enumerate(hots):
        rows += dot_nn(hot, amps_held[:, chunk * pao : (chunk + 1) * pao])
    made[block * width :, :] = rows.astype(BF16)
    send(block * width, tail)
    coming[1].wait()
    for j in range(block):
        coming[2 + j].wait()
        made[j * width : (j + 1) * width, :] = masked_rows(held[j], count_held[first + j])
        send(j * width, width)
    for copy in going:
        copy.wait()


def pack(panels, amps, count, block):
    pairs, width, pao = panels.shape
    chunks = width * width // pao
    rows = block * width + tail_rows(block, chunks)
    return pl.pallas_call(
        functools.partial(pack_kernel, block, width, chunks),
        out_shape=jax.ShapeDtypeStruct((rows, pao), BF16),
        in_specs=[whole(pltpu.HBM)] * 3,
        out_specs=whole(pltpu.HBM),
        scratch_shapes=[
            pltpu.VMEM((block, width, pao), BF16),
            pltpu.VMEM(amps.shape, BF16),
            pltpu.SMEM(count.shape, I32),
            pltpu.VMEM((rows, pao), BF16),
            pltpu.SemaphoreType.DMA((3 + 2 * block,)),
        ],
        compiler_params=pltpu.CompilerParams(vmem_limit_bytes=PACK_VMEM_BYTES),
        name="pack",
    )(panels, amps, count)


def local_kernel(
    block,
    width,
    ways,
    coupling,
    orbital,
    lmo,
    pos,
    fock,
    amps,
    energy,
    count,
    fit,
    panels,
    weight_in,
    weight_out,
    block_amps,
    own,
    masked,
    out,
    weight,
    fock_of,
    held,
    panels_held,
    count_held,
    both,
    sems,
):
    copies = [
        pltpu.make_async_copy(count, count_held, sems.at[0]),
        pltpu.make_async_copy(panels, panels_held, sems.at[1]),
    ]
    groups = fit.shape[0] // block
    fits = []
    for group in range(groups):
        part = pl.ds(group * block, block)
        fits.append(pltpu.make_async_copy(fit.at[part], held.at[part], sems.at[2 + group]))
    for copy in copies + fits:
        copy.start()
    total = pos.shape[1]
    occ = fock.shape[0]
    couplings = orbital.shape[0]
    per_dev = energy.shape[0]
    pair_devices = total // per_dev
    pair = lax.axis_index("pair")
    first = lax.axis_index("aux") * block
    here = pos[...] == iota((total, total), 0)
    label_at = jnp.sum(jnp.where(here, iota((total, total), 1), 0), axis=1, keepdims=True)
    level = iota((occ, total), 0)
    hot_i = (lmo[0:1, :] == level).astype(F32)
    hot_j = (lmo[1:2, :] == level).astype(F32)
    fock_of[0] = dot_nn(fock[...], hot_j, HIGHEST)
    fock_of[1] = lax.dot_general(
        fock[...], hot_i, (((0,), (0,)), ((), ())), precision=HIGHEST, preferred_element_type=F32
    )
    weight[...] = jnp.zeros_like(weight)

    def add(c, carry):
        hot_k = orbital[pl.ds(c, 1), :] == level
        for h in range(2):
            value = jnp.sum(jnp.where(hot_k, fock_of[h], 0.0), axis=0, keepdims=True)
            named = coupling[pl.ds(2 * c + h, 1), :] == label_at
            weight[...] += jnp.where(named, value, 0.0)
        return carry

    lax.fori_loop(0, couplings, add, 0, unroll=4)

    def of_pairs(rows, start):
        hot = (iota((rows, total), 1) == start + iota((rows, total), 0)).astype(F32)
        return dot_nt(hot, weight[...], HIGHEST)

    wide = per_dev * width
    thin = block * width
    wide_pair, wide_pno = lane_in(width, wide)
    thin_pair, _ = lane_in(width, thin)
    mine = of_pairs(per_dev, pair * per_dev)
    local = (iota((total, wide), 0) == pair * per_dev + wide_pair).astype(F32)
    for k in range(len(ways) + 1):
        start = pair
        if k > 0:
            start = jnp.int32(-pair_devices)
            for sender, receiver in ways[k - 1]:
                start = jnp.where(pair == receiver, sender, start)
        source = start * per_dev + first
        spread = (iota((total, thin), 0) == source + thin_pair).astype(F32)
        spread = dot_nn(mine, spread, HIGHEST)
        for group in range(groups):
            part = slice(group * block, (group + 1) * block)
            weight_in[k, group, :block, :] = spread[part, :]
        if k > 0:
            weight_out[k - 1] = dot_nn(of_pairs(8, source), local, HIGHEST)

    repeat = (iota((width, wide), 0) == wide_pno).astype(F32).astype(BF16)
    tiled = dot_nn(amps[...], repeat)
    row_pair, _ = row_in(width, wide)
    block_amps[...] = jnp.where(row_pair == wide_pair, tiled, 0.0).astype(BF16)

    for copy in copies:
        copy.wait()
    across = iota((occ, occ), 0) == iota((occ, occ), 1)
    diagonal = jnp.sum(jnp.where(across, fock[...], 0.0), axis=1, keepdims=True)
    gap_of = jnp.sum((hot_i + hot_j) * diagonal, axis=0, keepdims=True)
    row = iota((width, width), 0)
    column = iota((width, width), 1)
    for j in range(block):
        at = iota((1, total), 1) == pair * per_dev + first + j
        gap = jnp.sum(jnp.where(at, gap_of, 0.0), axis=1, keepdims=True)
        flat = energy[pl.ds(first + j, 1), :]
        upright = jnp.sum(jnp.where(row == column, flat, 0.0), axis=1, keepdims=True)
        live = count_held[first + j]
        values = amps[pl.ds((first + j) * width, width), :].astype(F32)
        term = (upright + flat - gap) * values
        own[:, j * width : (j + 1) * width] = jnp.where((row < live) & (column < live), term, 0.0)

    functions = held.shape[2]
    pao = held.shape[3]
    for p in range(per_dev):
        masked[p * width : (p + 1) * width, :] = masked_rows(panels_held[p], count_held[p])
    for group in range(groups):
        fits[group].wait()
        for p in range(group * block, (group + 1) * block):
            rows = slice(p * width, (p + 1) * width)
            if functions % 128 == 0:
                fitted = dot_nt(masked[rows, :], held[p].reshape(2 * functions, pao)).astype(BF16)
                both[0, rows, :] = fitted[:, :functions]
                both[1, rows, :] = fitted[:, functions:]
            else:
                for h in range(2):
                    both[h, rows, :] = dot_nt(masked[rows, :], held[p, h]).astype(BF16)
        rows = slice(group * thin, (group + 1) * thin)
        out[group] = fold_diagonal(dot_nt(both[0, rows, :], both[1, rows, :]), width)


def local(coupling, orbital, lmo, pos, fock, amps, energy, count, fit, panels, block, ways):
    rounds = len(ways)
    wide, width = amps.shape
    per_dev, _, pao = panels.shape
    total = pos.shape[1]
    occ = fock.shape[0]
    groups = per_dev // block
    thin = block * width
    return pl.pallas_call(
        functools.partial(local_kernel, block, width, ways),
        out_shape=(
            jax.ShapeDtypeStruct((rounds + 1, groups, 8, thin), F32),
            jax.ShapeDtypeStruct((rounds, 8, wide), F32),
            jax.ShapeDtypeStruct((wide, wide), BF16),
            jax.ShapeDtypeStruct((width, thin), F32),
            jax.ShapeDtypeStruct((wide, pao), BF16),
            jax.ShapeDtypeStruct((groups, width, thin), F32),
        ),
        in_specs=[whole()] * 7 + [whole(pltpu.HBM)] * 3,
        out_specs=(whole(),) * 6,
        scratch_shapes=[
            pltpu.VMEM((total, total), F32),
            pltpu.VMEM((2, occ, total), F32),
            pltpu.VMEM(fit.shape, BF16),
            pltpu.VMEM(panels.shape, BF16),
            pltpu.SMEM(count.shape, I32),
            pltpu.VMEM((2, wide, fit.shape[2]), BF16),
            pltpu.SemaphoreType.DMA((2 + groups,)),
        ],
        compiler_params=pltpu.CompilerParams(vmem_limit_bytes=LOCAL_VMEM_BYTES),
        cost_estimate=pl.CostEstimate(
            flops=6_000_000_000, bytes_accessed=fit.size * 2, transcendentals=0
        ),
        name="local",
    )(coupling, orbital, lmo, pos, fock, amps, energy, count, fit, panels)


def unpack_amps(sent, block, width):
    thin = block * width
    pao = sent.shape[1]
    per_chunk = pao // width
    row_pair, row_pno = row_in(width, thin)
    row_chunk = floor_div(row_pno, per_chunk)
    tail = sent.shape[0] - thin
    pick = (iota((thin, tail), 1) == row_chunk * block + row_pair).astype(F32).astype(BF16)
    picked = dot_nn(pick, sent[thin:, :])
    lane_block, _ = lane_in(width, pao)
    at = row_pno - per_chunk * row_chunk == lane_block
    picked = jnp.where(at, picked, 0.0).astype(BF16)
    _, down_pno = row_in(width, pao)
    across_pair, across_pno = lane_in(width, thin)
    fold = (down_pno == across_pno).astype(F32).astype(BF16)
    return jnp.where(row_pair == across_pair, dot_nn(picked, fold), 0.0).astype(BF16)


def scaled(half, weight, width):
    rows = half.shape[0] // width
    return jnp.concatenate(
        [half[t * width : (t + 1) * width, :] * weight[t : t + 1, :] for t in range(rows)], 0
    )


def add_in(block, width, masked, parts, put):
    thin = block * width
    inters, halves = [], []
    for sent, _ in parts:
        inter = dot_nt(masked[...], sent[:thin, :]).astype(BF16)
        half = dot_nn(inter, unpack_amps(sent, block, width)).astype(BF16).astype(F32)
        inters.append(inter)
        halves.append(half)
    for group in range(masked.shape[0] // thin):
        rows = slice(group * thin, (group + 1) * thin)
        square = jnp.zeros((thin, thin), F32)
        for (_, weight_in), inter, half in zip(parts, inters, halves):
            high, low = split_high_low(scaled(half[rows, :], weight_in[group], width))
            square += dot_nt(high, inter[rows, :]) + dot_nt(low, inter[rows, :])
        put(group, fold_diagonal(square, width))


def add_in_group(block, width, masked, sent, amps, weight_in, group):
    thin = block * width
    rows = pl.ds(pl.multiple_of(group * thin, thin), thin)
    inter = dot_nt(masked[rows, :], sent[:thin, :]).astype(BF16)
    half = dot_nn(inter, amps).astype(BF16).astype(F32)
    high, low = split_high_low(scaled(half, weight_in[group], width))
    return fold_diagonal(dot_nt(high, inter) + dot_nt(low, inter), width)


def add_back(block, width, sent, masked, block_amps, weight_out):
    thin = block * width
    inter = dot_nt(sent[:thin, :], masked[...]).astype(BF16)
    half = dot_nn(inter, block_amps[...]).astype(BF16).astype(F32)
    high, low = split_high_low(scaled(half, weight_out, width))
    return fold_diagonal(dot_nt(high, inter) + dot_nt(low, inter), width)


def both_kernel(block, width, *refs):
    masked, block_amps, acc, sent, weight_in, weight_out = refs[:6]
    out, back = refs[-2:]
    parts = [(sent, weight_in)] + ([refs[6:8]] if len(refs) > 8 else [])

    def put(group, value):
        out[group] = acc[group] - value

    back[...] = as_sent(add_back(block, width, sent, masked, block_amps, weight_out)).astype(BF16)
    add_in(block, width, masked, parts, put)


NEAR = 2


def far_kernel(block, width, sent, masked, block_amps, weight_out, weight_in, acc, back, *outs):
    amps = unpack_amps(sent, block, width)
    aux = lax.axis_index("aux")
    back[...] = as_sent(add_back(block, width, sent, masked, block_amps, weight_out)).astype(BF16)
    for k, out in enumerate(outs, NEAR):
        group = lax.bitwise_xor(aux, k)
        added = add_in_group(block, width, masked, sent, amps, weight_in, group)
        out[...] = as_sent(acc[group] - added).astype(BF16)


def near_kernel(block, width, returned, sent, masked, weight_in, acc, own, *refs):
    backs, outs = refs[:returned], refs[returned:]
    amps = unpack_amps(sent, block, width)
    aux = lax.axis_index("aux")
    for k, out in enumerate(outs):
        group = lax.bitwise_xor(aux, k)
        added = add_in_group(block, width, masked, sent, amps, weight_in, group)
        if k > 0:
            out[...] = as_sent(acc[group] - added).astype(BF16)
        else:
            mine = as_sent(acc[group] - added + own[...])
            for back in backs:
                mine -= back[...].astype(F32)
            out[...] = mine


def finish_kernel(block, width, count, *refs):
    parts, out, held = refs[:count], refs[count], refs[count + 1]
    total = parts[0][...]
    for n, part in enumerate(parts[1:]):
        value = part[...].astype(F32)
        total = total - value if n == 0 else total + value
    for s in range(block):
        for r in range(0, width, 16):
            lane = r // 16 * block * width + s * width
            held[s * width + r : s * width + r + 16, :] = total[:, lane : lane + width]
    for a in range(width):
        out[:, a * width : (a + 1) * width] = held[pl.ds(a, block, stride=width), :]


def as_sent(values):
    rows = values.shape[0]
    return jnp.concatenate([values[r : r + 16, :] for r in range(0, rows, 16)], 1)


def call(kernel, name, out_shape, args, flops, scratch=()):
    many = isinstance(out_shape, tuple)
    return pl.pallas_call(
        kernel,
        out_shape=out_shape,
        in_specs=[whole()] * len(args),
        out_specs=(whole(),) * len(out_shape) if many else whole(),
        scratch_shapes=list(scratch),
        compiler_params=pltpu.CompilerParams(vmem_limit_bytes=VMEM_BYTES),
        cost_estimate=pl.CostEstimate(flops=flops, bytes_accessed=3_000_000, transcendentals=0),
        name=name,
    )(*args)


def schedule(devices):
    if devices == 4:
        return [[(0, 2), (3, 1), (2, 3), (1, 0)], [(1, 2), (3, 0)]]
    rounds = []
    for k in range(1, devices // 2 + 1):
        whole_way = [(p, (p + k) % devices) for p in range(devices)]
        if 2 * k == devices:
            whole_way = [way for way in whole_way if (way[0] < k) == (way[0] % 2 == 0)]
        rounds.append(whole_way)
    return rounds


def completed(way, devices):
    idle = sorted(set(range(devices)) - {p for p, _ in way})
    open_ends = sorted(set(range(devices)) - {q for _, q in way})
    return way + list(zip(idle, open_ends))


def on_device(
    panels,
    amplitudes,
    fitted_ints,
    pno_energy,
    fock_occ,
    pno_count,
    pair_pos,
    coupling,
    coupling_lmo,
    pair_lmo,
):
    per_dev, width, pao = panels.shape
    pair_devices = lax.axis_size("pair")
    aux_devices = lax.axis_size("aux")
    block = per_dev // aux_devices
    thin = block * width
    couplings = coupling.shape[1]
    total = pair_pos.shape[0]
    ways = schedule(pair_devices)
    rounds = len(ways)
    back_ways = [completed([(q, p) for p, q in way], pair_devices) for way in ways]

    sent = pack(panels, amplitudes, pno_count, block)
    arrived = [lax.ppermute(sent, "pair", way) for way in ways]
    weight_in, weight_out, block_amps, own, masked, acc = local(
        coupling.transpose(1, 2, 0).reshape(2 * couplings, total),
        coupling_lmo.T,
        pair_lmo.T,
        pair_pos[None, :],
        fock_occ,
        amplitudes.reshape(per_dev * width, width),
        pno_energy,
        pno_count,
        fitted_ints,
        panels,
        block,
        ways,
    )

    acc_shape = jax.ShapeDtypeStruct(acc.shape, F32)
    own_shape = jax.ShapeDtypeStruct((16, width // 16 * thin), F32)
    block_shape = jax.ShapeDtypeStruct(own_shape.shape, BF16)
    flops = 1_000_000_000
    returned = []
    for k in range(1, rounds):
        args = (masked, block_amps, acc, arrived[k - 1], weight_in[k], weight_out[k - 1])
        if k == 1:
            args += (sent, weight_in[0])
        acc, back = call(
            functools.partial(both_kernel, block, width),
            "couple",
            (acc_shape, block_shape),
            args,
            2 * flops,
        )
        returned.append(lax.ppermute(back, "pair", back_ways[k - 1]))
    back, *far = call(
        functools.partial(far_kernel, block, width),
        "couple_far",
        (block_shape,) * (1 + aux_devices - NEAR),
        (arrived[-1], masked, block_amps, weight_out[-1], weight_in[rounds], acc),
        flops,
    )
    last_back = lax.ppermute(back, "pair", back_ways[-1])
    near = call(
        functools.partial(near_kernel, block, width, len(returned)),
        "couple_near",
        (own_shape,) + (block_shape,) * (NEAR - 1),
        (arrived[-1], masked, weight_in[rounds], acc, own, *returned),
        flops,
    )
    parts = list(near) + far
    sums = {0: last_back}
    for k in range(1, aux_devices):
        sums[k] = lax.ppermute(parts[k], "aux", [(d, d ^ k) for d in range(aux_devices)])
    order = [0, 2, 3]
    order += [k for k in range(1, aux_devices) if k not in order]
    sums = [parts[0]] + [sums[k] for k in order]
    return call(
        functools.partial(finish_kernel, block, width, len(sums)),
        "finish",
        jax.ShapeDtypeStruct((block, width * width), F32),
        tuple(sums),
        1_000_000,
        [pltpu.VMEM((thin, width), F32)],
    )


def solution(mesh):
    placed = (
        P(("groups", "pair"), None, None),
        P(("groups", "pair"), None),
        P(("groups", "pair"), None, "aux", None),
        P(("groups", "pair"), None),
        P("groups", None),
        P(("groups", "pair")),
        P("groups"),
        P("groups", None, None),
        P("groups", None),
        P("groups", None),
    )
    return jax.shard_map(
        on_device,
        mesh=mesh,
        in_specs=placed,
        out_specs=P(("groups", "pair", "aux"), None),
        check_vma=False,
    )
```

```python
import functools

import jax
import jax.numpy as jnp
from jax import lax
from jax.experimental import pallas as pl
from jax.experimental.pallas import tpu as pltpu
from jax.sharding import PartitionSpec as P

BF16 = jnp.bfloat16
F32 = jnp.float32
I32 = jnp.int32
HIGHEST = lax.Precision.HIGHEST
VMEM_BYTES = 48 * 1024 * 1024
PACK_VMEM_BYTES = 61 * 1024 * 1024
LOCAL_VMEM_BYTES = 48 * 1024 * 1024


def dot_nn(a, b, precision=None):
    return lax.dot_general(
        a, b, (((1,), (0,)), ((), ())), precision=precision, preferred_element_type=F32
    )


def dot_nt(a, b, precision=None):
    return lax.dot_general(
        a, b, (((1,), (1,)), ((), ())), precision=precision, preferred_element_type=F32
    )


def iota(shape, dim):
    return lax.broadcasted_iota(I32, shape, dim)


def floor_div(values, by):
    return jnp.floor((values.astype(F32) + 0.5) * (1.0 / by)).astype(I32)


def whole(memory_space=pltpu.VMEM):
    return pl.BlockSpec(memory_space=memory_space)


def lane_in(width, lanes):
    lane = iota((1, lanes), 1)
    block = floor_div(lane, width)
    return block, lane - width * block


def row_in(width, rows):
    row = iota((rows, 1), 0)
    block = floor_div(row, width)
    return block, row - width * block


def fold_diagonal(square, width):
    lanes = square.shape[1]
    block, _ = lane_in(width, lanes)
    out = jnp.zeros((width, lanes), F32)
    for n in range(lanes // width):
        out += jnp.where(block == n, square[n * width : (n + 1) * width, :], 0.0)
    return out


def tail_rows(block, chunks):
    return -(-(block * chunks) // 16) * 16


def masked_rows(panel, count):
    live = iota(panel.shape, 0) < count
    return jnp.where(live, panel.astype(F32), 0.0).astype(BF16)


def split_high_low(values):
    high = values.astype(BF16)
    return high, (values - high.astype(F32)).astype(BF16)


def pack_kernel(block, width, chunks, panels, amps, count, out, held, amps_held, count_held, made, sems):
    first = lax.axis_index("aux") * block
    coming = [
        pltpu.make_async_copy(amps, amps_held, sems.at[0]),
        pltpu.make_async_copy(count, count_held, sems.at[1]),
    ]
    for j in range(block):
        coming.append(pltpu.make_async_copy(panels.at[first + j], held.at[j], sems.at[2 + j]))
    for copy in coming:
        copy.start()
    pao = held.shape[2]
    pairs = amps_held.shape[0]
    tail = tail_rows(block, chunks)
    row = iota((tail, pairs), 0)
    source = iota((tail, pairs), 1)
    hots = []
    for chunk in range(chunks):
        inside = (row >= chunk * block) & (row < (chunk + 1) * block)
        hots.append((inside & (source == first + row - chunk * block)).astype(F32).astype(BF16))
    going = []

    def send(start, rows):
        part = pl.ds(start, rows)
        sem = sems.at[2 + block + len(going)]
        going.append(pltpu.make_async_copy(made.at[part], out.at[part], sem))
        going[-1].start()

    coming[0].wait()
    rows = jnp.zeros((tail, pao), F32)
    for chunk, hot in enumerate(hots):
        rows += dot_nn(hot, amps_held[:, chunk * pao : (chunk + 1) * pao])
    made[block * width :, :] = rows.astype(BF16)
    send(block * width, tail)
    coming[1].wait()
    for j in range(block):
        coming[2 + j].wait()
        made[j * width : (j + 1) * width, :] = masked_rows(held[j], count_held[first + j])
        send(j * width, width)
    for copy in going:
        copy.wait()


def pack(panels, amps, count, block):
    pairs, width, pao = panels.shape
    chunks = width * width // pao
    rows = block * width + tail_rows(block, chunks)
    return pl.pallas_call(
        functools.partial(pack_kernel, block, width, chunks),
        out_shape=jax.ShapeDtypeStruct((rows, pao), BF16),
        in_specs=[whole(pltpu.HBM)] * 3,
        out_specs=whole(pltpu.HBM),
        scratch_shapes=[
            pltpu.VMEM((block, width, pao), BF16),
            pltpu.VMEM(amps.shape, BF16),
            pltpu.SMEM(count.shape, I32),
            pltpu.VMEM((rows, pao), BF16),
            pltpu.SemaphoreType.DMA((3 + 2 * block,)),
        ],
        compiler_params=pltpu.CompilerParams(vmem_limit_bytes=PACK_VMEM_BYTES),
        name="pack",
    )(panels, amps, count)


def local_kernel(
    block,
    width,
    ways,
    coupling,
    orbital,
    lmo,
    pos,
    fock,
    amps,
    energy,
    count,
    fit,
    panels,
    weight_in,
    weight_out,
    block_amps,
    own,
    masked,
    out,
    weight,
    fock_of,
    held,
    panels_held,
    count_held,
    both,
    sems,
):
    copies = [
        pltpu.make_async_copy(count, count_held, sems.at[0]),
        pltpu.make_async_copy(panels, panels_held, sems.at[1]),
    ]
    groups = fit.shape[0] // block
    fits = []
    for group in range(groups):
        part = pl.ds(group * block, block)
        fits.append(pltpu.make_async_copy(fit.at[part], held.at[part], sems.at[2 + group]))
    for copy in copies + fits:
        copy.start()
    total = pos.shape[1]
    occ = fock.shape[0]
    couplings = orbital.shape[0]
    per_dev = energy.shape[0]
    pair_devices = total // per_dev
    wide = per_dev * width
    thin = block * width
    functions = held.shape[2]
    pao = held.shape[3]
    pair = lax.axis_index("pair")
    first = lax.axis_index("aux") * block
    level = iota((occ, total), 0)
    hot_i = (lmo[0:1, :] == level).astype(F32)
    hot_j = (lmo[1:2, :] == level).astype(F32)

    def weights_of_targets():
        here = pos[...] == iota((total, total), 0)
        label_at = jnp.sum(jnp.where(here, iota((total, total), 1), 0), axis=1, keepdims=True)
        fock_of[0] = dot_nn(fock[...], hot_j, HIGHEST)
        fock_of[1] = lax.dot_general(
            fock[...], hot_i, (((0,), (0,)), ((), ())), precision=HIGHEST, preferred_element_type=F32
        )

        def add(c, value):
            hot_k = orbital[pl.ds(c, 1), :] == level
            for h in range(2):
                fock_k = jnp.sum(jnp.where(hot_k, fock_of[h], 0.0), axis=0, keepdims=True)
                named = coupling[pl.ds(2 * c + h, 1), :] == label_at
                value = value + jnp.where(named, fock_k, 0.0)
            return value

        if total <= 128:
            value = jnp.zeros((total, total), F32)
            for c in range(couplings):
                value = add(c, value)
            weight[...] = value
        else:
            weight[...] = jnp.zeros_like(weight)

            def step(c, carry):
                weight[...] = add(c, weight[...])
                return carry

            lax.fori_loop(0, couplings, step, 0)

    def spread_weights():
        def of_pairs(rows, start):
            hot = (iota((rows, total), 1) == start + iota((rows, total), 0)).astype(F32)
            return dot_nt(hot, weight[...], HIGHEST)

        wide_pair, _ = lane_in(width, wide)
        thin_pair, _ = lane_in(width, thin)
        mine = of_pairs(per_dev, pair * per_dev)
        local = (iota((total, wide), 0) == pair * per_dev + wide_pair).astype(F32)
        for k in range(len(ways) + 1):
            start = pair
            if k > 0:
                start = jnp.int32(-pair_devices)
                for sender, receiver in ways[k - 1]:
                    start = jnp.where(pair == receiver, sender, start)
            source = start * per_dev + first
            spread = (iota((total, thin), 0) == source + thin_pair).astype(F32)
            spread = dot_nn(mine, spread, HIGHEST)
            for group in range(groups):
                part = slice(group * block, (group + 1) * block)
                weight_in[k, group, :block, :] = spread[part, :]
            if k > 0:
                weight_out[k - 1] = dot_nn(of_pairs(8, source), local, HIGHEST)

    def amplitudes_and_energies():
        wide_pair, wide_pno = lane_in(width, wide)
        repeat = (iota((width, wide), 0) == wide_pno).astype(F32).astype(BF16)
        tiled = dot_nn(amps[...], repeat)
        row_pair, _ = row_in(width, wide)
        block_amps[...] = jnp.where(row_pair == wide_pair, tiled, 0.0).astype(BF16)
        across = iota((occ, occ), 0) == iota((occ, occ), 1)
        diagonal = jnp.sum(jnp.where(across, fock[...], 0.0), axis=1, keepdims=True)
        gap_of = jnp.sum((hot_i + hot_j) * diagonal, axis=0, keepdims=True)
        row = iota((width, width), 0)
        column = iota((width, width), 1)
        for j in range(block):
            at = iota((1, total), 1) == pair * per_dev + first + j
            gap = jnp.sum(jnp.where(at, gap_of, 0.0), axis=1, keepdims=True)
            flat = energy[pl.ds(first + j, 1), :]
            upright = jnp.sum(jnp.where(row == column, flat, 0.0), axis=1, keepdims=True)
            live = count_held[first + j]
            values = amps[pl.ds((first + j) * width, width), :].astype(F32)
            inside = (row < live) & (column < live)
            lanes = slice(j * width, (j + 1) * width)
            own[:, lanes] = jnp.where(inside, (upright + flat - gap) * values, 0.0)

    def masked_panels():
        for copy in copies:
            copy.wait()
        for p in range(per_dev):
            masked[p * width : (p + 1) * width, :] = masked_rows(panels_held[p], count_held[p])

    def exchange(group):
        for p in range(group * block, (group + 1) * block):
            rows = slice(p * width, (p + 1) * width)
            if functions % 128 == 0:
                fitted = dot_nt(masked[rows, :], held[p].reshape(2 * functions, pao)).astype(BF16)
                both[0, rows, :] = fitted[:, :functions]
                both[1, rows, :] = fitted[:, functions:]
            else:
                for h in range(2):
                    both[h, rows, :] = dot_nt(masked[rows, :], held[p, h]).astype(BF16)
        rows = slice(group * thin, (group + 1) * thin)
        out[group] = fold_diagonal(dot_nt(both[0, rows, :], both[1, rows, :]), width)

    beside = [weights_of_targets, spread_weights, amplitudes_and_energies]
    beside.pop(0)()
    beside.pop(0)()
    masked_panels()
    for group in range(groups):
        fits[group].wait()
        exchange(group)
        if beside:
            beside.pop(0)()
    for piece in beside:
        piece()


def local(coupling, orbital, lmo, pos, fock, amps, energy, count, fit, panels, block, ways):
    rounds = len(ways)
    wide, width = amps.shape
    per_dev, _, pao = panels.shape
    total = pos.shape[1]
    occ = fock.shape[0]
    groups = per_dev // block
    thin = block * width
    return pl.pallas_call(
        functools.partial(local_kernel, block, width, ways),
        out_shape=(
            jax.ShapeDtypeStruct((rounds + 1, groups, 8, thin), F32),
            jax.ShapeDtypeStruct((rounds, 8, wide), F32),
            jax.ShapeDtypeStruct((wide, wide), BF16),
            jax.ShapeDtypeStruct((width, thin), F32),
            jax.ShapeDtypeStruct((wide, pao), BF16),
            jax.ShapeDtypeStruct((groups, width, thin), F32),
        ),
        in_specs=[whole()] * 7 + [whole(pltpu.HBM)] * 3,
        out_specs=(whole(),) * 6,
        scratch_shapes=[
            pltpu.VMEM((total, total), F32),
            pltpu.VMEM((2, occ, total), F32),
            pltpu.VMEM(fit.shape, BF16),
            pltpu.VMEM(panels.shape, BF16),
            pltpu.SMEM(count.shape, I32),
            pltpu.VMEM((2, wide, fit.shape[2]), BF16),
            pltpu.SemaphoreType.DMA((2 + groups,)),
        ],
        compiler_params=pltpu.CompilerParams(vmem_limit_bytes=LOCAL_VMEM_BYTES),
        cost_estimate=pl.CostEstimate(
            flops=6_000_000_000, bytes_accessed=fit.size * 2, transcendentals=0
        ),
        name="local",
    )(coupling, orbital, lmo, pos, fock, amps, energy, count, fit, panels)


def unpack_amps(sent, block, width):
    thin = block * width
    pao = sent.shape[1]
    per_chunk = pao // width
    row_pair, row_pno = row_in(width, thin)
    row_chunk = floor_div(row_pno, per_chunk)
    tail = sent.shape[0] - thin
    pick = (iota((thin, tail), 1) == row_chunk * block + row_pair).astype(F32).astype(BF16)
    picked = dot_nn(pick, sent[thin:, :])
    lane_block, _ = lane_in(width, pao)
    at = row_pno - per_chunk * row_chunk == lane_block
    picked = jnp.where(at, picked, 0.0).astype(BF16)
    _, down_pno = row_in(width, pao)
    across_pair, across_pno = lane_in(width, thin)
    fold = (down_pno == across_pno).astype(F32).astype(BF16)
    return jnp.where(row_pair == across_pair, dot_nn(picked, fold), 0.0).astype(BF16)


def scaled(half, weight, width):
    rows = half.shape[0] // width
    return jnp.concatenate(
        [half[t * width : (t + 1) * width, :] * weight[t : t + 1, :] for t in range(rows)], 0
    )


def add_in(block, width, masked, parts, put):
    thin = block * width
    inters, halves = [], []
    for sent, _ in parts:
        inter = dot_nt(masked[...], sent[:thin, :]).astype(BF16)
        half = dot_nn(inter, unpack_amps(sent, block, width)).astype(BF16).astype(F32)
        inters.append(inter)
        halves.append(half)
    for group in range(masked.shape[0] // thin):
        rows = slice(group * thin, (group + 1) * thin)
        square = jnp.zeros((thin, thin), F32)
        for (_, weight_in), inter, half in zip(parts, inters, halves):
            high, low = split_high_low(scaled(half[rows, :], weight_in[group], width))
            square += dot_nt(high, inter[rows, :]) + dot_nt(low, inter[rows, :])
        put(group, fold_diagonal(square, width))


def add_in_group(block, width, masked, sent, amps, weight_in, group):
    thin = block * width
    rows = pl.ds(pl.multiple_of(group * thin, thin), thin)
    inter = dot_nt(masked[rows, :], sent[:thin, :]).astype(BF16)
    half = dot_nn(inter, amps).astype(BF16).astype(F32)
    high, low = split_high_low(scaled(half, weight_in[group], width))
    return fold_diagonal(dot_nt(high, inter) + dot_nt(low, inter), width)


def add_back(block, width, sent, masked, block_amps, weight_out):
    thin = block * width
    inter = dot_nt(sent[:thin, :], masked[...]).astype(BF16)
    half = dot_nn(inter, block_amps[...]).astype(BF16).astype(F32)
    high, low = split_high_low(scaled(half, weight_out, width))
    return fold_diagonal(dot_nt(high, inter) + dot_nt(low, inter), width)


def both_kernel(block, width, *refs):
    masked, block_amps, acc, sent, weight_in, weight_out = refs[:6]
    out, back = refs[-2:]
    parts = [(sent, weight_in)] + ([refs[6:8]] if len(refs) > 8 else [])

    def put(group, value):
        out[group] = acc[group] - value

    back[...] = as_sent(add_back(block, width, sent, masked, block_amps, weight_out)).astype(BF16)
    add_in(block, width, masked, parts, put)


NEAR = 2


def far_kernel(block, width, sent, masked, block_amps, weight_out, weight_in, acc, back, *outs):
    amps = unpack_amps(sent, block, width)
    aux = lax.axis_index("aux")
    back[...] = as_sent(add_back(block, width, sent, masked, block_amps, weight_out)).astype(BF16)
    for k, out in enumerate(outs, NEAR):
        group = lax.bitwise_xor(aux, k)
        added = add_in_group(block, width, masked, sent, amps, weight_in, group)
        out[...] = as_sent(acc[group] - added).astype(BF16)


def near_kernel(block, width, returned, sent, masked, weight_in, acc, own, *refs):
    backs, outs = refs[:returned], refs[returned:]
    amps = unpack_amps(sent, block, width)
    aux = lax.axis_index("aux")
    for k, out in enumerate(outs):
        group = lax.bitwise_xor(aux, k)
        added = add_in_group(block, width, masked, sent, amps, weight_in, group)
        if k > 0:
            out[...] = as_sent(acc[group] - added).astype(BF16)
        else:
            mine = as_sent(acc[group] - added + own[...])
            for back in backs:
                mine -= back[...].astype(F32)
            out[...] = mine


def finish_kernel(block, width, count, *refs):
    parts, out, held = refs[:count], refs[count], refs[count + 1]
    total = parts[0][...]
    for n, part in enumerate(parts[1:]):
        value = part[...].astype(F32)
        total = total - value if n == 0 else total + value
    for s in range(block):
        for r in range(0, width, 16):
            lane = r // 16 * block * width + s * width
            held[s * width + r : s * width + r + 16, :] = total[:, lane : lane + width]
    for a in range(width):
        out[:, a * width : (a + 1) * width] = held[pl.ds(a, block, stride=width), :]


def as_sent(values):
    rows = values.shape[0]
    return jnp.concatenate([values[r : r + 16, :] for r in range(0, rows, 16)], 1)


def call(kernel, name, out_shape, args, flops, scratch=()):
    many = isinstance(out_shape, tuple)
    return pl.pallas_call(
        kernel,
        out_shape=out_shape,
        in_specs=[whole()] * len(args),
        out_specs=(whole(),) * len(out_shape) if many else whole(),
        scratch_shapes=list(scratch),
        compiler_params=pltpu.CompilerParams(vmem_limit_bytes=VMEM_BYTES),
        cost_estimate=pl.CostEstimate(flops=flops, bytes_accessed=3_000_000, transcendentals=0),
        name=name,
    )(*args)


def schedule(devices):
    if devices == 4:
        return [[(0, 2), (3, 1), (2, 3), (1, 0)], [(1, 2), (3, 0)]]
    rounds = []
    for k in range(1, devices // 2 + 1):
        whole_way = [(p, (p + k) % devices) for p in range(devices)]
        if 2 * k == devices:
            whole_way = [way for way in whole_way if (way[0] < k) == (way[0] % 2 == 0)]
        rounds.append(whole_way)
    return rounds


def completed(way, devices):
    idle = sorted(set(range(devices)) - {p for p, _ in way})
    open_ends = sorted(set(range(devices)) - {q for _, q in way})
    return way + list(zip(idle, open_ends))


def on_device(
    panels,
    amplitudes,
    fitted_ints,
    pno_energy,
    fock_occ,
    pno_count,
    pair_pos,
    coupling,
    coupling_lmo,
    pair_lmo,
):
    per_dev, width, pao = panels.shape
    pair_devices = lax.axis_size("pair")
    aux_devices = lax.axis_size("aux")
    block = per_dev // aux_devices
    thin = block * width
    couplings = coupling.shape[1]
    total = pair_pos.shape[0]
    ways = schedule(pair_devices)
    rounds = len(ways)
    back_ways = [completed([(q, p) for p, q in way], pair_devices) for way in ways]

    sent = pack(panels, amplitudes, pno_count, block)
    arrived = [lax.ppermute(sent, "pair", way) for way in ways]
    weight_in, weight_out, block_amps, own, masked, acc = local(
        coupling.transpose(1, 2, 0).reshape(2 * couplings, total),
        coupling_lmo.T,
        pair_lmo.T,
        pair_pos[None, :],
        fock_occ,
        amplitudes.reshape(per_dev * width, width),
        pno_energy,
        pno_count,
        fitted_ints,
        panels,
        block,
        ways,
    )

    acc_shape = jax.ShapeDtypeStruct(acc.shape, F32)
    own_shape = jax.ShapeDtypeStruct((16, width // 16 * thin), F32)
    block_shape = jax.ShapeDtypeStruct(own_shape.shape, BF16)
    flops = 1_000_000_000
    returned = []
    for k in range(1, rounds):
        args = (masked, block_amps, acc, arrived[k - 1], weight_in[k], weight_out[k - 1])
        if k == 1:
            args += (sent, weight_in[0])
        acc, back = call(
            functools.partial(both_kernel, block, width),
            "couple",
            (acc_shape, block_shape),
            args,
            2 * flops,
        )
        returned.append(lax.ppermute(back, "pair", back_ways[k - 1]))
    back, *far = call(
        functools.partial(far_kernel, block, width),
        "couple_far",
        (block_shape,) * (1 + aux_devices - NEAR),
        (arrived[-1], masked, block_amps, weight_out[-1], weight_in[rounds], acc),
        flops,
    )
    last_back = lax.ppermute(back, "pair", back_ways[-1])
    near = call(
        functools.partial(near_kernel, block, width, len(returned)),
        "couple_near",
        (own_shape,) + (block_shape,) * (NEAR - 1),
        (arrived[-1], masked, weight_in[rounds], acc, own, *returned),
        flops,
    )
    parts = list(near) + far
    sums = {0: last_back}
    for k in range(1, aux_devices):
        sums[k] = lax.ppermute(parts[k], "aux", [(d, d ^ k) for d in range(aux_devices)])
    order = [0, 3, 2]
    order += [k for k in range(1, aux_devices) if k not in order]
    sums = [parts[0]] + [sums[k] for k in order]
    return call(
        functools.partial(finish_kernel, block, width, len(sums)),
        "finish",
        jax.ShapeDtypeStruct((block, width * width), F32),
        tuple(sums),
        1_000_000,
        [pltpu.VMEM((thin, width), F32)],
    )


def solution(mesh):
    placed = (
        P(("groups", "pair"), None, None),
        P(("groups", "pair"), None),
        P(("groups", "pair"), None, "aux", None),
        P(("groups", "pair"), None),
        P("groups", None),
        P(("groups", "pair")),
        P("groups"),
        P("groups", None, None),
        P("groups", None),
        P("groups", None),
    )
    return jax.shard_map(
        on_device,
        mesh=mesh,
        in_specs=placed,
        out_specs=P(("groups", "pair", "aux"), None),
        check_vma=False,
    )
```

```python
import functools

import jax
import jax.numpy as jnp
from jax import lax
from jax.experimental import pallas as pl
from jax.experimental.pallas import tpu as pltpu
from jax.sharding import PartitionSpec as P

BF16 = jnp.bfloat16
F32 = jnp.float32
I32 = jnp.int32
HIGHEST = lax.Precision.HIGHEST
VMEM_BYTES = 48 * 1024 * 1024
PACK_VMEM_BYTES = 61 * 1024 * 1024
LOCAL_VMEM_BYTES = 48 * 1024 * 1024


def dot_nn(a, b, precision=None):
    return lax.dot_general(
        a, b, (((1,), (0,)), ((), ())), precision=precision, preferred_element_type=F32
    )


def dot_nt(a, b, precision=None):
    return lax.dot_general(
        a, b, (((1,), (1,)), ((), ())), precision=precision, preferred_element_type=F32
    )


def iota(shape, dim):
    return lax.broadcasted_iota(I32, shape, dim)


def floor_div(values, by):
    return jnp.floor((values.astype(F32) + 0.5) * (1.0 / by)).astype(I32)


def whole(memory_space=pltpu.VMEM):
    return pl.BlockSpec(memory_space=memory_space)


def lane_in(width, lanes):
    lane = iota((1, lanes), 1)
    block = floor_div(lane, width)
    return block, lane - width * block


def row_in(width, rows):
    row = iota((rows, 1), 0)
    block = floor_div(row, width)
    return block, row - width * block


def fold_diagonal(square, width):
    lanes = square.shape[1]
    block, _ = lane_in(width, lanes)
    out = jnp.zeros((width, lanes), F32)
    for n in range(lanes // width):
        out += jnp.where(block == n, square[n * width : (n + 1) * width, :], 0.0)
    return out


def tail_rows(block, chunks):
    return -(-(block * chunks) // 16) * 16


def masked_rows(panel, count):
    live = iota(panel.shape, 0) < count
    return jnp.where(live, panel.astype(F32), 0.0).astype(BF16)


def split_high_low(values):
    high = values.astype(BF16)
    return high, (values - high.astype(F32)).astype(BF16)


def pack_kernel(block, width, chunks, panels, amps, count, out, held, amps_held, count_held, made, sems):
    first = lax.axis_index("aux") * block
    coming = [
        pltpu.make_async_copy(amps, amps_held, sems.at[0]),
        pltpu.make_async_copy(count, count_held, sems.at[1]),
    ]
    for j in range(block):
        coming.append(pltpu.make_async_copy(panels.at[first + j], held.at[j], sems.at[2 + j]))
    for copy in coming:
        copy.start()
    pao = held.shape[2]
    pairs = amps_held.shape[0]
    tail = tail_rows(block, chunks)
    row = iota((tail, pairs), 0)
    source = iota((tail, pairs), 1)
    hots = []
    for chunk in range(chunks):
        inside = (row >= chunk * block) & (row < (chunk + 1) * block)
        hots.append((inside & (source == first + row - chunk * block)).astype(F32).astype(BF16))
    going = []

    def send(start, rows):
        part = pl.ds(start, rows)
        sem = sems.at[2 + block + len(going)]
        going.append(pltpu.make_async_copy(made.at[part], out.at[part], sem))
        going[-1].start()

    coming[0].wait()
    rows = jnp.zeros((tail, pao), F32)
    for chunk, hot in enumerate(hots):
        rows += dot_nn(hot, amps_held[:, chunk * pao : (chunk + 1) * pao])
    made[block * width :, :] = rows.astype(BF16)
    send(block * width, tail)
    coming[1].wait()
    for j in range(block):
        coming[2 + j].wait()
        made[j * width : (j + 1) * width, :] = masked_rows(held[j], count_held[first + j])
        send(j * width, width)
    for copy in going:
        copy.wait()


def pack(panels, amps, count, block):
    pairs, width, pao = panels.shape
    chunks = width * width // pao
    rows = block * width + tail_rows(block, chunks)
    return pl.pallas_call(
        functools.partial(pack_kernel, block, width, chunks),
        out_shape=jax.ShapeDtypeStruct((rows, pao), BF16),
        in_specs=[whole(pltpu.HBM)] * 3,
        out_specs=whole(pltpu.HBM),
        scratch_shapes=[
            pltpu.VMEM((block, width, pao), BF16),
            pltpu.VMEM(amps.shape, BF16),
            pltpu.SMEM(count.shape, I32),
            pltpu.VMEM((rows, pao), BF16),
            pltpu.SemaphoreType.DMA((3 + 2 * block,)),
        ],
        compiler_params=pltpu.CompilerParams(vmem_limit_bytes=PACK_VMEM_BYTES),
        name="pack",
    )(panels, amps, count)


def local_kernel(
    block,
    width,
    ways,
    coupling,
    orbital,
    lmo,
    pos,
    fock,
    amps,
    energy,
    count,
    fit,
    panels,
    weight_in,
    weight_out,
    block_amps,
    own,
    masked,
    out,
    weight,
    fock_of,
    held,
    panels_held,
    count_held,
    both,
    sems,
):
    copies = [
        pltpu.make_async_copy(count, count_held, sems.at[0]),
        pltpu.make_async_copy(panels, panels_held, sems.at[1]),
    ]
    groups = fit.shape[0] // block
    fits = []
    for group in range(groups):
        part = pl.ds(group * block, block)
        fits.append(pltpu.make_async_copy(fit.at[part], held.at[part], sems.at[2 + group]))
    for copy in copies + fits:
        copy.start()
    total = pos.shape[1]
    occ = fock.shape[0]
    couplings = orbital.shape[0]
    per_dev = energy.shape[0]
    pair_devices = total // per_dev
    wide = per_dev * width
    thin = block * width
    functions = held.shape[2]
    pao = held.shape[3]
    pair = lax.axis_index("pair")
    first = lax.axis_index("aux") * block
    level = iota((occ, total), 0)
    hot_i = (lmo[0:1, :] == level).astype(F32)
    hot_j = (lmo[1:2, :] == level).astype(F32)

    def weights_of_targets():
        here = pos[...] == iota((total, total), 0)
        label_at = jnp.sum(jnp.where(here, iota((total, total), 1), 0), axis=1, keepdims=True)
        fock_of[0] = dot_nn(fock[...], hot_j, HIGHEST)
        fock_of[1] = lax.dot_general(
            fock[...], hot_i, (((0,), (0,)), ((), ())), precision=HIGHEST, preferred_element_type=F32
        )

        def add(c, value):
            hot_k = orbital[pl.ds(c, 1), :] == level
            for h in range(2):
                fock_k = jnp.sum(jnp.where(hot_k, fock_of[h], 0.0), axis=0, keepdims=True)
                named = coupling[pl.ds(2 * c + h, 1), :] == label_at
                value = value + jnp.where(named, fock_k, 0.0)
            return value

        if total <= 128:
            value = jnp.zeros((total, total), F32)
            for c in range(couplings):
                value = add(c, value)
            weight[...] = value
        else:
            weight[...] = jnp.zeros_like(weight)

            def step(c, carry):
                weight[...] = add(c, weight[...])
                return carry

            lax.fori_loop(0, couplings, step, 0)

    def spread_weights():
        def of_pairs(rows, start):
            hot = (iota((rows, total), 1) == start + iota((rows, total), 0)).astype(F32)
            return dot_nt(hot, weight[...], HIGHEST)

        wide_pair, _ = lane_in(width, wide)
        thin_pair, _ = lane_in(width, thin)
        mine = of_pairs(per_dev, pair * per_dev)
        local = (iota((total, wide), 0) == pair * per_dev + wide_pair).astype(F32)
        for k in range(len(ways) + 1):
            start = pair
            if k > 0:
                start = jnp.int32(-pair_devices)
                for sender, receiver in ways[k - 1]:
                    start = jnp.where(pair == receiver, sender, start)
            source = start * per_dev + first
            spread = (iota((total, thin), 0) == source + thin_pair).astype(F32)
            spread = dot_nn(mine, spread, HIGHEST)
            for group in range(groups):
                part = slice(group * block, (group + 1) * block)
                weight_in[k, group, :block, :] = spread[part, :]
            if k > 0:
                weight_out[k - 1] = dot_nn(of_pairs(8, source), local, HIGHEST)

    def amplitudes_and_energies():
        wide_pair, wide_pno = lane_in(width, wide)
        repeat = (iota((width, wide), 0) == wide_pno).astype(F32).astype(BF16)
        tiled = dot_nn(amps[...], repeat)
        row_pair, _ = row_in(width, wide)
        block_amps[...] = jnp.where(row_pair == wide_pair, tiled, 0.0).astype(BF16)
        across = iota((occ, occ), 0) == iota((occ, occ), 1)
        diagonal = jnp.sum(jnp.where(across, fock[...], 0.0), axis=1, keepdims=True)
        gap_of = jnp.sum((hot_i + hot_j) * diagonal, axis=0, keepdims=True)
        row = iota((width, width), 0)
        column = iota((width, width), 1)
        for j in range(block):
            at = iota((1, total), 1) == pair * per_dev + first + j
            gap = jnp.sum(jnp.where(at, gap_of, 0.0), axis=1, keepdims=True)
            flat = energy[pl.ds(first + j, 1), :]
            upright = jnp.sum(jnp.where(row == column, flat, 0.0), axis=1, keepdims=True)
            live = count_held[first + j]
            values = amps[pl.ds((first + j) * width, width), :].astype(F32)
            inside = (row < live) & (column < live)
            lanes = slice(j * width, (j + 1) * width)
            own[:, lanes] = jnp.where(inside, (upright + flat - gap) * values, 0.0)

    def masked_panels():
        for copy in copies:
            copy.wait()
        for p in range(per_dev):
            masked[p * width : (p + 1) * width, :] = masked_rows(panels_held[p], count_held[p])

    def exchange(group):
        for p in range(group * block, (group + 1) * block):
            rows = slice(p * width, (p + 1) * width)
            if functions % 128 == 0:
                fitted = dot_nt(masked[rows, :], held[p].reshape(2 * functions, pao)).astype(BF16)
                both[0, rows, :] = fitted[:, :functions]
                both[1, rows, :] = fitted[:, functions:]
            else:
                for h in range(2):
                    both[h, rows, :] = dot_nt(masked[rows, :], held[p, h]).astype(BF16)
        rows = slice(group * thin, (group + 1) * thin)
        out[group] = fold_diagonal(dot_nt(both[0, rows, :], both[1, rows, :]), width)

    beside = [weights_of_targets, spread_weights, amplitudes_and_energies]
    beside.pop(0)()
    beside.pop(0)()
    masked_panels()
    for group in range(groups):
        fits[group].wait()
        exchange(group)
        if beside:
            beside.pop(0)()
    for piece in beside:
        piece()


def local(coupling, orbital, lmo, pos, fock, amps, energy, count, fit, panels, block, ways):
    rounds = len(ways)
    wide, width = amps.shape
    per_dev, _, pao = panels.shape
    total = pos.shape[1]
    occ = fock.shape[0]
    groups = per_dev // block
    thin = block * width
    return pl.pallas_call(
        functools.partial(local_kernel, block, width, ways),
        out_shape=(
            jax.ShapeDtypeStruct((rounds + 1, groups, 8, thin), F32),
            jax.ShapeDtypeStruct((rounds, 8, wide), F32),
            jax.ShapeDtypeStruct((wide, wide), BF16),
            jax.ShapeDtypeStruct((width, thin), F32),
            jax.ShapeDtypeStruct((wide, pao), BF16),
            jax.ShapeDtypeStruct((groups, width, thin), F32),
        ),
        in_specs=[whole()] * 7 + [whole(pltpu.HBM)] * 3,
        out_specs=(whole(),) * 6,
        scratch_shapes=[
            pltpu.VMEM((total, total), F32),
            pltpu.VMEM((2, occ, total), F32),
            pltpu.VMEM(fit.shape, BF16),
            pltpu.VMEM(panels.shape, BF16),
            pltpu.SMEM(count.shape, I32),
            pltpu.VMEM((2, wide, fit.shape[2]), BF16),
            pltpu.SemaphoreType.DMA((2 + groups,)),
        ],
        compiler_params=pltpu.CompilerParams(vmem_limit_bytes=LOCAL_VMEM_BYTES),
        cost_estimate=pl.CostEstimate(
            flops=6_000_000_000, bytes_accessed=fit.size * 2, transcendentals=0
        ),
        name="local",
    )(coupling, orbital, lmo, pos, fock, amps, energy, count, fit, panels)


def unpack_amps(sent, block, width):
    thin = block * width
    pao = sent.shape[1]
    per_chunk = pao // width
    row_pair, row_pno = row_in(width, thin)
    row_chunk = floor_div(row_pno, per_chunk)
    tail = sent.shape[0] - thin
    pick = (iota((thin, tail), 1) == row_chunk * block + row_pair).astype(F32).astype(BF16)
    picked = dot_nn(pick, sent[thin:, :])
    lane_block, _ = lane_in(width, pao)
    at = row_pno - per_chunk * row_chunk == lane_block
    picked = jnp.where(at, picked, 0.0).astype(BF16)
    _, down_pno = row_in(width, pao)
    across_pair, across_pno = lane_in(width, thin)
    fold = (down_pno == across_pno).astype(F32).astype(BF16)
    return jnp.where(row_pair == across_pair, dot_nn(picked, fold), 0.0).astype(BF16)


def scaled(half, weight, width):
    rows = half.shape[0] // width
    return jnp.concatenate(
        [half[t * width : (t + 1) * width, :] * weight[t : t + 1, :] for t in range(rows)], 0
    )


def add_in(block, width, masked, parts, put):
    thin = block * width
    inters, halves = [], []
    for sent, _ in parts:
        inter = dot_nt(masked[...], sent[:thin, :]).astype(BF16)
        half = dot_nn(inter, unpack_amps(sent, block, width)).astype(BF16).astype(F32)
        inters.append(inter)
        halves.append(half)
    for group in range(masked.shape[0] // thin):
        rows = slice(group * thin, (group + 1) * thin)
        square = jnp.zeros((thin, thin), F32)
        for (_, weight_in), inter, half in zip(parts, inters, halves):
            high, low = split_high_low(scaled(half[rows, :], weight_in[group], width))
            square += dot_nt(high, inter[rows, :]) + dot_nt(low, inter[rows, :])
        put(group, fold_diagonal(square, width))


def add_in_two(block, width, masked, sent, amps, weight_in, away):
    thin = block * width
    aux = lax.axis_index("aux")
    odd = lax.bitwise_and(aux, 1)
    base = lax.bitwise_xor(aux, away) - odd
    rows = pl.ds(pl.multiple_of(base * thin, thin), 2 * thin)
    inter = dot_nt(masked[rows, :], sent[:thin, :]).astype(BF16)
    half = dot_nn(inter, amps).astype(BF16).astype(F32)
    added = []
    for n in range(2):
        part = slice(n * thin, (n + 1) * thin)
        high, low = split_high_low(scaled(half[part, :], weight_in[base + n], width))
        square = dot_nt(high, inter[part, :])
        added.append(fold_diagonal(square, width))
    first, second = added
    return jnp.where(odd == 0, first, second), jnp.where(odd == 0, second, first)


def add_back(block, width, sent, masked, block_amps, weight_out):
    thin = block * width
    inter = dot_nt(sent[:thin, :], masked[...]).astype(BF16)
    half = dot_nn(inter, block_amps[...]).astype(BF16).astype(F32)
    high, low = split_high_low(scaled(half, weight_out, width))
    return fold_diagonal(dot_nt(high, inter), width)


def both_kernel(block, width, *refs):
    masked, block_amps, acc, sent, weight_in, weight_out = refs[:6]
    out, back = refs[-2:]
    parts = [(sent, weight_in)] + ([refs[6:8]] if len(refs) > 8 else [])

    def put(group, value):
        out[group] = acc[group] - value

    back[...] = as_sent(add_back(block, width, sent, masked, block_amps, weight_out)).astype(BF16)
    add_in(block, width, masked, parts, put)


NEAR = 2


def far_kernel(block, width, sent, masked, block_amps, weight_out, weight_in, acc, back, *outs):
    amps = unpack_amps(sent, block, width)
    aux = lax.axis_index("aux")
    back[...] = as_sent(add_back(block, width, sent, masked, block_amps, weight_out)).astype(BF16)
    for k in range(0, len(outs), 2):
        added = add_in_two(block, width, masked, sent, amps, weight_in, NEAR + k)
        for n in range(2):
            group = lax.bitwise_xor(aux, NEAR + k + n)
            outs[k + n][...] = as_sent(acc[group] - added[n]).astype(BF16)


def near_kernel(block, width, returned, sent, masked, weight_in, acc, own, *refs):
    backs, outs = refs[:returned], refs[returned:]
    amps = unpack_amps(sent, block, width)
    aux = lax.axis_index("aux")
    added = add_in_two(block, width, masked, sent, amps, weight_in, 0)
    mine = as_sent(acc[aux] - added[0] + own[...])
    for back in backs:
        mine -= back[...].astype(F32)
    outs[0][...] = mine
    outs[1][...] = as_sent(acc[lax.bitwise_xor(aux, 1)] - added[1]).astype(BF16)


def finish_kernel(block, width, count, *refs):
    parts, out, held = refs[:count], refs[count], refs[count + 1]
    total = parts[0][...]
    for n, part in enumerate(parts[1:]):
        value = part[...].astype(F32)
        total = total - value if n == 0 else total + value
    for s in range(block):
        for r in range(0, width, 16):
            lane = r // 16 * block * width + s * width
            held[s * width + r : s * width + r + 16, :] = total[:, lane : lane + width]
    for a in range(width):
        out[:, a * width : (a + 1) * width] = held[pl.ds(a, block, stride=width), :]


def as_sent(values):
    rows = values.shape[0]
    return jnp.concatenate([values[r : r + 16, :] for r in range(0, rows, 16)], 1)


def call(kernel, name, out_shape, args, flops, scratch=()):
    many = isinstance(out_shape, tuple)
    return pl.pallas_call(
        kernel,
        out_shape=out_shape,
        in_specs=[whole()] * len(args),
        out_specs=(whole(),) * len(out_shape) if many else whole(),
        scratch_shapes=list(scratch),
        compiler_params=pltpu.CompilerParams(vmem_limit_bytes=VMEM_BYTES),
        cost_estimate=pl.CostEstimate(flops=flops, bytes_accessed=3_000_000, transcendentals=0),
        name=name,
    )(*args)


def schedule(devices):
    if devices == 4:
        return [[(0, 2), (3, 1), (2, 3), (1, 0)], [(1, 2), (3, 0)]]
    rounds = []
    for k in range(1, devices // 2 + 1):
        whole_way = [(p, (p + k) % devices) for p in range(devices)]
        if 2 * k == devices:
            whole_way = [way for way in whole_way if (way[0] < k) == (way[0] % 2 == 0)]
        rounds.append(whole_way)
    return rounds


def completed(way, devices):
    idle = sorted(set(range(devices)) - {p for p, _ in way})
    open_ends = sorted(set(range(devices)) - {q for _, q in way})
    return way + list(zip(idle, open_ends))


def on_device(
    panels,
    amplitudes,
    fitted_ints,
    pno_energy,
    fock_occ,
    pno_count,
    pair_pos,
    coupling,
    coupling_lmo,
    pair_lmo,
):
    per_dev, width, pao = panels.shape
    pair_devices = lax.axis_size("pair")
    aux_devices = lax.axis_size("aux")
    block = per_dev // aux_devices
    thin = block * width
    couplings = coupling.shape[1]
    total = pair_pos.shape[0]
    ways = schedule(pair_devices)
    rounds = len(ways)
    back_ways = [completed([(q, p) for p, q in way], pair_devices) for way in ways]

    sent = pack(panels, amplitudes, pno_count, block)
    arrived = [lax.ppermute(sent, "pair", way) for way in ways]
    weight_in, weight_out, block_amps, own, masked, acc = local(
        coupling.transpose(1, 2, 0).reshape(2 * couplings, total),
        coupling_lmo.T,
        pair_lmo.T,
        pair_pos[None, :],
        fock_occ,
        amplitudes.reshape(per_dev * width, width),
        pno_energy,
        pno_count,
        fitted_ints,
        panels,
        block,
        ways,
    )

    acc_shape = jax.ShapeDtypeStruct(acc.shape, F32)
    own_shape = jax.ShapeDtypeStruct((16, width // 16 * thin), F32)
    block_shape = jax.ShapeDtypeStruct(own_shape.shape, BF16)
    flops = 1_000_000_000
    returned = []
    for k in range(1, rounds):
        args = (masked, block_amps, acc, arrived[k - 1], weight_in[k], weight_out[k - 1])
        if k == 1:
            args += (sent, weight_in[0])
        acc, back = call(
            functools.partial(both_kernel, block, width),
            "couple",
            (acc_shape, block_shape),
            args,
            2 * flops,
        )
        returned.append(lax.ppermute(back, "pair", back_ways[k - 1]))
    back, *far = call(
        functools.partial(far_kernel, block, width),
        "couple_far",
        (block_shape,) * (1 + aux_devices - NEAR),
        (arrived[-1], masked, block_amps, weight_out[-1], weight_in[rounds], acc),
        flops,
    )
    last_back = lax.ppermute(back, "pair", back_ways[-1])
    near = call(
        functools.partial(near_kernel, block, width, len(returned)),
        "couple_near",
        (own_shape,) + (block_shape,) * (NEAR - 1),
        (arrived[-1], masked, weight_in[rounds], acc, own, *returned),
        flops,
    )
    parts = list(near) + far
    sums = {0: last_back}
    for k in range(1, aux_devices):
        sums[k] = lax.ppermute(parts[k], "aux", [(d, d ^ k) for d in range(aux_devices)])
    order = [0, 3, 2]
    order += [k for k in range(1, aux_devices) if k not in order]
    sums = [parts[0]] + [sums[k] for k in order]
    return call(
        functools.partial(finish_kernel, block, width, len(sums)),
        "finish",
        jax.ShapeDtypeStruct((block, width * width), F32),
        tuple(sums),
        1_000_000,
        [pltpu.VMEM((thin, width), F32)],
    )


def solution(mesh):
    placed = (
        P(("groups", "pair"), None, None),
        P(("groups", "pair"), None),
        P(("groups", "pair"), None, "aux", None),
        P(("groups", "pair"), None),
        P("groups", None),
        P(("groups", "pair")),
        P("groups"),
        P("groups", None, None),
        P("groups", None),
        P("groups", None),
    )
    return jax.shard_map(
        on_device,
        mesh=mesh,
        in_specs=placed,
        out_specs=P(("groups", "pair", "aux"), None),
        check_vma=False,
    )
```

```python
import functools

import jax
import jax.numpy as jnp
from jax import lax
from jax.experimental import pallas as pl
from jax.experimental.pallas import tpu as pltpu
from jax.sharding import PartitionSpec as P

BF16 = jnp.bfloat16
F32 = jnp.float32
I32 = jnp.int32
HIGHEST = lax.Precision.HIGHEST
VMEM_BYTES = 48 * 1024 * 1024
PACK_VMEM_BYTES = 61 * 1024 * 1024
LOCAL_VMEM_BYTES = 48 * 1024 * 1024


def dot_nn(a, b, precision=None):
    return lax.dot_general(
        a, b, (((1,), (0,)), ((), ())), precision=precision, preferred_element_type=F32
    )


def dot_nt(a, b, precision=None):
    return lax.dot_general(
        a, b, (((1,), (1,)), ((), ())), precision=precision, preferred_element_type=F32
    )


def iota(shape, dim):
    return lax.broadcasted_iota(I32, shape, dim)


def floor_div(values, by):
    return jnp.floor((values.astype(F32) + 0.5) * (1.0 / by)).astype(I32)


def whole(memory_space=pltpu.VMEM):
    return pl.BlockSpec(memory_space=memory_space)


def lane_in(width, lanes):
    lane = iota((1, lanes), 1)
    block = floor_div(lane, width)
    return block, lane - width * block


def row_in(width, rows):
    row = iota((rows, 1), 0)
    block = floor_div(row, width)
    return block, row - width * block


def fold_diagonal(square, width):
    lanes = square.shape[1]
    block, _ = lane_in(width, lanes)
    out = jnp.zeros((width, lanes), F32)
    for n in range(lanes // width):
        out += jnp.where(block == n, square[n * width : (n + 1) * width, :], 0.0)
    return out


def tail_rows(block, chunks):
    return -(-(block * chunks) // 16) * 16


def masked_rows(panel, count):
    live = iota(panel.shape, 0) < count
    return jnp.where(live, panel.astype(F32), 0.0).astype(BF16)


def rounded(values):
    return values.astype(BF16)


def pack_kernel(block, width, chunks, panels, amps, count, out, rows_out, held, amps_held, count_held, sems):
    first = lax.axis_index("aux") * block
    coming = [
        pltpu.make_async_copy(count, count_held, sems.at[0]),
        pltpu.make_async_copy(amps, amps_held, sems.at[1]),
        pltpu.make_async_copy(panels.at[pl.ds(first, block)], held, sems.at[2]),
    ]
    for copy in coming:
        copy.start()
    pao = held.shape[2]
    pairs = amps_held.shape[0]
    tail = tail_rows(block, chunks)
    row = iota((tail, pairs), 0)
    source = iota((tail, pairs), 1)
    line = iota((tail, 1), 0)
    chunk_of = floor_div(line, block)
    lane_pno, column = lane_in(width, pao)
    coming[0].wait()
    live = jnp.zeros((tail, 1), I32)
    for j in range(block):
        live = jnp.where(line - block * chunk_of == j, count_held[first + j], live)
    pno = chunk_of * (pao // width) + lane_pno
    coming[1].wait()
    rows = jnp.zeros((tail, pao), F32)
    for chunk in range(chunks):
        inside = (row >= chunk * block) & (row < (chunk + 1) * block)
        hot = (inside & (source == first + row - chunk * block)).astype(F32).astype(BF16)
        rows += dot_nn(hot, amps_held[:, chunk * pao : (chunk + 1) * pao])
    rows = jnp.where((pno < live) & (column < live), rows, 0.0).astype(BF16)
    out[block * width :, :] = rows
    rows_out[...] = rows
    coming[2].wait()
    for j in range(block):
        out[j * width : (j + 1) * width, :] = masked_rows(held[j], count_held[first + j])


def pack(panels, amps, count, block):
    pairs, width, pao = panels.shape
    chunks = width * width // pao
    tail = tail_rows(block, chunks)
    return pl.pallas_call(
        functools.partial(pack_kernel, block, width, chunks),
        out_shape=(
            jax.ShapeDtypeStruct((block * width + tail, pao), BF16),
            jax.ShapeDtypeStruct((tail, pao), BF16),
        ),
        in_specs=[whole(pltpu.HBM)] * 3,
        out_specs=(whole(),) * 2,
        scratch_shapes=[
            pltpu.VMEM((block, width, pao), BF16),
            pltpu.VMEM(amps.shape, BF16),
            pltpu.SMEM(count.shape, I32),
            pltpu.SemaphoreType.DMA((3,)),
        ],
        compiler_params=pltpu.CompilerParams(vmem_limit_bytes=PACK_VMEM_BYTES),
        name="pack",
    )(panels, amps, count)


def local_kernel(
    block,
    width,
    ways,
    coupling,
    orbital,
    lmo,
    pos,
    fock,
    amps,
    energy,
    count,
    fit,
    panels,
    weight_in,
    weight_out,
    block_amps,
    own,
    live_out,
    masked,
    out,
    weight,
    fock_of,
    held,
    panels_held,
    count_held,
    both,
    sems,
):
    copies = [
        pltpu.make_async_copy(count, count_held, sems.at[0]),
        pltpu.make_async_copy(panels, panels_held, sems.at[1]),
    ]
    groups = fit.shape[0] // block
    fits = []
    parts = [(group * block, block) for group in range(groups - 1)]
    half = block // 2
    parts += [((groups - 1) * block, half), ((groups - 1) * block + half, block - half)]
    for start, size in parts:
        part = pl.ds(start, size)
        sem = sems.at[2 + len(fits)]
        fits.append(pltpu.make_async_copy(fit.at[part], held.at[part], sem))
    for copy in copies + fits:
        copy.start()
    total = pos.shape[1]
    occ = fock.shape[0]
    couplings = orbital.shape[0]
    per_dev = energy.shape[0]
    pair_devices = total // per_dev
    wide = per_dev * width
    thin = block * width
    functions = held.shape[2]
    pao = held.shape[3]
    pair = lax.axis_index("pair")
    first = lax.axis_index("aux") * block
    level = iota((occ, total), 0)
    hot_i = (lmo[0:1, :] == level).astype(F32)
    hot_j = (lmo[1:2, :] == level).astype(F32)

    def weights_of_targets():
        here = pos[...] == iota((total, total), 0)
        label_at = jnp.sum(jnp.where(here, iota((total, total), 1), 0), axis=1, keepdims=True)
        fock_of[0] = dot_nn(fock[...], hot_j, HIGHEST)
        fock_of[1] = lax.dot_general(
            fock[...], hot_i, (((0,), (0,)), ((), ())), precision=HIGHEST, preferred_element_type=F32
        )

        def add(c, value):
            hot_k = orbital[pl.ds(c, 1), :] == level
            for h in range(2):
                fock_k = jnp.sum(jnp.where(hot_k, fock_of[h], 0.0), axis=0, keepdims=True)
                named = coupling[pl.ds(2 * c + h, 1), :] == label_at
                value = value + jnp.where(named, fock_k, 0.0)
            return value

        if total <= 128:
            value = jnp.zeros((total, total), F32)
            for c in range(couplings):
                value = add(c, value)
            weight[...] = value
        else:
            weight[...] = jnp.zeros_like(weight)

            def step(c, carry):
                weight[...] = add(c, weight[...])
                return carry

            lax.fori_loop(0, couplings, step, 0)

    def spread_weights():
        def of_pairs(rows, start):
            hot = (iota((rows, total), 1) == start + iota((rows, total), 0)).astype(F32)
            return dot_nt(hot, weight[...], HIGHEST)

        wide_pair, _ = lane_in(width, wide)
        thin_pair, _ = lane_in(width, thin)
        mine = of_pairs(per_dev, pair * per_dev)
        local = (iota((total, wide), 0) == pair * per_dev + wide_pair).astype(F32)
        for k in range(len(ways) + 1):
            start = pair
            if k > 0:
                start = jnp.int32(-pair_devices)
                for sender, receiver in ways[k - 1]:
                    start = jnp.where(pair == receiver, sender, start)
            source = start * per_dev + first
            spread = (iota((total, thin), 0) == source + thin_pair).astype(F32)
            spread = dot_nn(mine, spread, HIGHEST)
            for group in range(groups):
                part = slice(group * block, (group + 1) * block)
                weight_in[k, group, :block, :] = spread[part, :]
            if k > 0:
                weight_out[k - 1] = dot_nn(of_pairs(8, source), local, HIGHEST)

    def amplitudes_and_energies():
        wide_pair, wide_pno = lane_in(width, wide)
        repeat = (iota((width, wide), 0) == wide_pno).astype(F32).astype(BF16)
        tiled = dot_nn(amps[...], repeat)
        row_pair, _ = row_in(width, wide)
        block_amps[...] = jnp.where(row_pair == wide_pair, tiled, 0.0).astype(BF16)
        across = iota((occ, occ), 0) == iota((occ, occ), 1)
        diagonal = jnp.sum(jnp.where(across, fock[...], 0.0), axis=1, keepdims=True)
        gap_of = jnp.sum((hot_i + hot_j) * diagonal, axis=0, keepdims=True)
        row = iota((width, width), 0)
        column = iota((width, width), 1)
        for j in range(block):
            at = iota((1, total), 1) == pair * per_dev + first + j
            gap = jnp.sum(jnp.where(at, gap_of, 0.0), axis=1, keepdims=True)
            flat = energy[pl.ds(first + j, 1), :]
            upright = jnp.sum(jnp.where(row == column, flat, 0.0), axis=1, keepdims=True)
            live = count_held[first + j]
            values = amps[pl.ds((first + j) * width, width), :].astype(F32)
            inside = (row < live) & (column < live)
            lanes = slice(j * width, (j + 1) * width)
            own[:, lanes] = jnp.where(inside, (upright + flat - gap) * values, 0.0)
            live_out[:, lanes] = inside.astype(F32)

    def masked_panels():
        for copy in copies:
            copy.wait()
        for p in range(per_dev):
            masked[p * width : (p + 1) * width, :] = masked_rows(panels_held[p], count_held[p])

    def exchange(group):
        for p in range(group * block, (group + 1) * block):
            if p == parts[-1][0]:
                fits[-1].wait()
            rows = slice(p * width, (p + 1) * width)
            if functions % 128 == 0:
                fitted = dot_nt(masked[rows, :], held[p].reshape(2 * functions, pao)).astype(BF16)
                both[0, rows, :] = fitted[:, :functions]
                both[1, rows, :] = fitted[:, functions:]
            else:
                for h in range(2):
                    both[h, rows, :] = dot_nt(masked[rows, :], held[p, h]).astype(BF16)
        rows = slice(group * thin, (group + 1) * thin)
        out[group] = fold_diagonal(dot_nt(both[0, rows, :], both[1, rows, :]), width)

    beside = [weights_of_targets, spread_weights, amplitudes_and_energies]
    beside.pop(0)()
    beside.pop(0)()
    masked_panels()
    for group in range(groups):
        fits[group].wait()
        exchange(group)
        if beside:
            beside.pop(0)()
    for piece in beside:
        piece()


def local(coupling, orbital, lmo, pos, fock, amps, energy, count, fit, panels, block, ways):
    rounds = len(ways)
    wide, width = amps.shape
    per_dev, _, pao = panels.shape
    total = pos.shape[1]
    occ = fock.shape[0]
    groups = per_dev // block
    thin = block * width
    return pl.pallas_call(
        functools.partial(local_kernel, block, width, ways),
        out_shape=(
            jax.ShapeDtypeStruct((rounds + 1, groups, 8, thin), F32),
            jax.ShapeDtypeStruct((rounds, 8, wide), F32),
            jax.ShapeDtypeStruct((wide, wide), BF16),
            jax.ShapeDtypeStruct((width, thin), F32),
            jax.ShapeDtypeStruct((width, thin), F32),
            jax.ShapeDtypeStruct((wide, pao), BF16),
            jax.ShapeDtypeStruct((groups, width, thin), F32),
        ),
        in_specs=[whole()] * 7 + [whole(pltpu.HBM)] * 3,
        out_specs=(whole(),) * 7,
        scratch_shapes=[
            pltpu.VMEM((total, total), F32),
            pltpu.VMEM((2, occ, total), F32),
            pltpu.VMEM(fit.shape, BF16),
            pltpu.VMEM(panels.shape, BF16),
            pltpu.SMEM(count.shape, I32),
            pltpu.VMEM((2, wide, fit.shape[2]), BF16),
            pltpu.SemaphoreType.DMA((3 + groups,)),
        ],
        compiler_params=pltpu.CompilerParams(vmem_limit_bytes=LOCAL_VMEM_BYTES),
        cost_estimate=pl.CostEstimate(
            flops=6_000_000_000, bytes_accessed=fit.size * 2, transcendentals=0
        ),
        name="local",
    )(coupling, orbital, lmo, pos, fock, amps, energy, count, fit, panels)


def unpack_amps(rows, block, width):
    thin = block * width
    tail, pao = rows.shape
    per_chunk = pao // width
    row_pair, row_pno = row_in(width, thin)
    row_chunk = floor_div(row_pno, per_chunk)
    pick = (iota((thin, tail), 1) == row_chunk * block + row_pair).astype(F32).astype(BF16)
    picked = dot_nn(pick, rows[...])
    lane_block, _ = lane_in(width, pao)
    at = row_pno - per_chunk * row_chunk == lane_block
    picked = jnp.where(at, picked, 0.0).astype(BF16)
    _, down_pno = row_in(width, pao)
    across_pair, across_pno = lane_in(width, thin)
    fold = (down_pno == across_pno).astype(F32).astype(BF16)
    return jnp.where(row_pair == across_pair, dot_nn(picked, fold), 0.0).astype(BF16)


def scaled(half, weight, width):
    rows = half.shape[0] // width
    return jnp.concatenate(
        [half[t * width : (t + 1) * width, :] * weight[t : t + 1, :] for t in range(rows)], 0
    )


def add_in(block, width, masked, parts, put):
    thin = block * width
    inters, halves = [], []
    for sent, rows, _ in parts:
        inter = dot_nt(masked[...], sent[:thin, :]).astype(BF16)
        half = dot_nn(inter, unpack_amps(rows, block, width)).astype(BF16).astype(F32)
        inters.append(inter)
        halves.append(half)
    for group in range(masked.shape[0] // thin):
        rows = slice(group * thin, (group + 1) * thin)
        square = jnp.zeros((thin, thin), F32)
        for (_, _, weight_in), inter, half in zip(parts, inters, halves):
            high = rounded(scaled(half[rows, :], weight_in[group], width))
            square += dot_nt(high, inter[rows, :])
        put(group, fold_diagonal(square, width))


def add_in_two(block, width, masked, sent, amps, weight_in, away):
    thin = block * width
    aux = lax.axis_index("aux")
    odd = lax.bitwise_and(aux, 1)
    base = lax.bitwise_xor(aux, away) - odd
    rows = pl.ds(pl.multiple_of(base * thin, thin), 2 * thin)
    inter = dot_nt(masked[rows, :], sent[:thin, :]).astype(BF16)
    half = dot_nn(inter, amps).astype(BF16).astype(F32)
    added = []
    for n in range(2):
        part = slice(n * thin, (n + 1) * thin)
        high = rounded(scaled(half[part, :], weight_in[base + n], width))
        square = dot_nt(high, inter[part, :])
        added.append(fold_diagonal(square, width))
    first, second = added
    return jnp.where(odd == 0, first, second), jnp.where(odd == 0, second, first)


def add_back(block, width, sent, masked, block_amps, weight_out):
    thin = block * width
    inter = dot_nt(sent[:thin, :], masked[...]).astype(BF16)
    half = dot_nn(inter, block_amps[...]).astype(BF16).astype(F32)
    high = rounded(scaled(half, weight_out, width))
    return fold_diagonal(dot_nt(high, inter), width)


def both_kernel(block, width, *refs):
    masked, block_amps, acc, weight_out, sent, rows, weight_in = refs[:7]
    out, back = refs[-2:]
    parts = [(sent, rows, weight_in)]
    if len(refs) > 9:
        own, own_weight = refs[7:9]
        parts.append((own, own.at[block * width :], own_weight))

    def put(group, value):
        out[group] = acc[group] - value

    back[...] = as_sent(add_back(block, width, sent, masked, block_amps, weight_out)).astype(BF16)
    add_in(block, width, masked, parts, put)


NEAR = 2


def far_kernel(block, width, sent, masked, block_amps, weight_out, weight_in, acc, back, *outs):
    amps = unpack_amps(sent.at[block * width :], block, width)
    aux = lax.axis_index("aux")
    back[...] = as_sent(add_back(block, width, sent, masked, block_amps, weight_out)).astype(BF16)
    for k in range(0, len(outs), 2):
        added = add_in_two(block, width, masked, sent, amps, weight_in, NEAR + k)
        for n in range(2):
            group = lax.bitwise_xor(aux, NEAR + k + n)
            outs[k + n][...] = as_sent(acc[group] - added[n]).astype(BF16)


def near_kernel(block, width, returned, sent, masked, weight_in, acc, own, live, *refs):
    backs, outs = refs[:returned], refs[returned:]
    amps = unpack_amps(sent.at[block * width :], block, width)
    aux = lax.axis_index("aux")
    added = add_in_two(block, width, masked, sent, amps, weight_in, 0)
    mine = as_sent(acc[aux] - added[0] + own[...])
    inside = as_sent(live[...]) > 0
    for back in backs:
        mine -= jnp.where(inside, back[...].astype(F32), 0.0)
    outs[0][...] = mine
    outs[1][...] = as_sent(acc[lax.bitwise_xor(aux, 1)] - added[1]).astype(BF16)


def finish_kernel(block, width, count, *refs):
    parts, out, held = refs[:count], refs[count], refs[count + 1]
    total = parts[0][...]
    for n, part in enumerate(parts[1:]):
        value = part[...].astype(F32)
        total = total - value if n == 0 else total + value
    for s in range(block):
        for r in range(0, width, 16):
            lane = r // 16 * block * width + s * width
            held[s * width + r : s * width + r + 16, :] = total[:, lane : lane + width]
    for a in range(width):
        out[:, a * width : (a + 1) * width] = held[pl.ds(a, block, stride=width), :]


def as_sent(values):
    rows = values.shape[0]
    return jnp.concatenate([values[r : r + 16, :] for r in range(0, rows, 16)], 1)


def call(kernel, name, out_shape, args, flops, scratch=()):
    many = isinstance(out_shape, tuple)
    return pl.pallas_call(
        kernel,
        out_shape=out_shape,
        in_specs=[whole()] * len(args),
        out_specs=(whole(),) * len(out_shape) if many else whole(),
        scratch_shapes=list(scratch),
        compiler_params=pltpu.CompilerParams(vmem_limit_bytes=VMEM_BYTES),
        cost_estimate=pl.CostEstimate(flops=flops, bytes_accessed=3_000_000, transcendentals=0),
        name=name,
    )(*args)


def schedule(devices):
    if devices == 4:
        return [[(0, 2), (3, 1), (2, 3), (1, 0)], [(2, 1), (0, 3)]]
    rounds = []
    for k in range(1, devices // 2 + 1):
        whole_way = [(p, (p + k) % devices) for p in range(devices)]
        if 2 * k == devices:
            whole_way = [way for way in whole_way if (way[0] < k) == (way[0] % 2 == 0)]
        rounds.append(whole_way)
    return rounds


def completed(way, devices):
    idle = sorted(set(range(devices)) - {p for p, _ in way})
    open_ends = sorted(set(range(devices)) - {q for _, q in way})
    return way + list(zip(idle, open_ends))


def on_device(
    panels,
    amplitudes,
    fitted_ints,
    pno_energy,
    fock_occ,
    pno_count,
    pair_pos,
    coupling,
    coupling_lmo,
    pair_lmo,
):
    per_dev, width, pao = panels.shape
    pair_devices = lax.axis_size("pair")
    aux_devices = lax.axis_size("aux")
    block = per_dev // aux_devices
    thin = block * width
    couplings = coupling.shape[1]
    total = pair_pos.shape[0]
    ways = schedule(pair_devices)
    rounds = len(ways)
    aux = lax.axis_index("aux")
    back_ways = [completed([(q, p) for p, q in way], pair_devices) for way in ways]

    raw = lax.dynamic_slice_in_dim(panels, aux * block, block, 0).reshape(thin, pao)
    full_ways = [completed(way, pair_devices) for way in ways]
    arrived = [lax.ppermute(raw, "pair", way) for way in full_ways[:-1]]
    sent, rows = pack(panels, amplitudes, pno_count, block)
    last = lax.ppermute(sent, "pair", full_ways[-1])
    rows = [lax.ppermute(rows, "pair", way) for way in full_ways[:-1]]
    arrived = list(zip(arrived, rows))

    weight_in, weight_out, block_amps, own, live, masked, acc = local(
        coupling.transpose(1, 2, 0).reshape(2 * couplings, total),
        coupling_lmo.T,
        pair_lmo.T,
        pair_pos[None, :],
        fock_occ,
        amplitudes.reshape(per_dev * width, width),
        pno_energy,
        pno_count,
        fitted_ints,
        panels,
        block,
        ways,
    )

    acc_shape = jax.ShapeDtypeStruct(acc.shape, F32)
    own_shape = jax.ShapeDtypeStruct((16, width // 16 * thin), F32)
    block_shape = jax.ShapeDtypeStruct(own_shape.shape, BF16)
    flops = 1_000_000_000
    returned = []
    for k in range(1, rounds):
        args = (masked, block_amps, acc, weight_out[k - 1], *arrived[k - 1], weight_in[k])
        if k == 1:
            args += (sent, weight_in[0])
        acc, back = call(
            functools.partial(both_kernel, block, width),
            "couple",
            (acc_shape, block_shape),
            args,
            2 * flops,
        )
        returned.append(lax.ppermute(back, "pair", back_ways[k - 1]))
    back, *far = call(
        functools.partial(far_kernel, block, width),
        "couple_far",
        (block_shape,) * (1 + aux_devices - NEAR),
        (last, masked, block_amps, weight_out[-1], weight_in[rounds], acc),
        flops,
    )
    last_back = lax.ppermute(back, "pair", back_ways[-1])
    near = call(
        functools.partial(near_kernel, block, width, len(returned)),
        "couple_near",
        (own_shape,) + (block_shape,) * (NEAR - 1),
        (last, masked, weight_in[rounds], acc, own, live, *returned),
        flops,
    )
    parts = list(near) + far
    sums = {0: last_back}
    for k in range(1, aux_devices):
        sums[k] = lax.ppermute(parts[k], "aux", [(d, d ^ k) for d in range(aux_devices)])
    order = [0, 3, 2]
    order += [k for k in range(1, aux_devices) if k not in order]
    sums = [parts[0]] + [sums[k] for k in order]
    return call(
        functools.partial(finish_kernel, block, width, len(sums)),
        "finish",
        jax.ShapeDtypeStruct((block, width * width), F32),
        tuple(sums),
        1_000_000,
        [pltpu.VMEM((thin, width), F32)],
    )


def solution(mesh):
    placed = (
        P(("groups", "pair"), None, None),
        P(("groups", "pair"), None),
        P(("groups", "pair"), None, "aux", None),
        P(("groups", "pair"), None),
        P("groups", None),
        P(("groups", "pair")),
        P("groups"),
        P("groups", None, None),
        P("groups", None),
        P("groups", None),
    )
    return jax.shard_map(
        on_device,
        mesh=mesh,
        in_specs=placed,
        out_specs=P(("groups", "pair", "aux"), None),
        check_vma=False,
    )
```

```python
import functools

import jax
import jax.numpy as jnp
from jax import lax
from jax.experimental import pallas as pl
from jax.experimental.pallas import tpu as pltpu
from jax.sharding import PartitionSpec as P

BF16 = jnp.bfloat16
F32 = jnp.float32
I32 = jnp.int32
HIGHEST = lax.Precision.HIGHEST
VMEM_BYTES = 48 * 1024 * 1024
PACK_VMEM_BYTES = 63 * 1024 * 1024
LOCAL_VMEM_BYTES = 48 * 1024 * 1024


def dot_nn(a, b, precision=None):
    return lax.dot_general(
        a, b, (((1,), (0,)), ((), ())), precision=precision, preferred_element_type=F32
    )


def dot_nt(a, b, precision=None):
    return lax.dot_general(
        a, b, (((1,), (1,)), ((), ())), precision=precision, preferred_element_type=F32
    )


def iota(shape, dim):
    return lax.broadcasted_iota(I32, shape, dim)


def floor_div(values, by):
    return jnp.floor((values.astype(F32) + 0.5) * (1.0 / by)).astype(I32)


def whole(memory_space=pltpu.VMEM):
    return pl.BlockSpec(memory_space=memory_space)


def lane_in(width, lanes):
    lane = iota((1, lanes), 1)
    block = floor_div(lane, width)
    return block, lane - width * block


def row_in(width, rows):
    row = iota((rows, 1), 0)
    block = floor_div(row, width)
    return block, row - width * block


def fold_diagonal(square, width):
    lanes = square.shape[1]
    block, _ = lane_in(width, lanes)
    out = jnp.zeros((width, lanes), F32)
    for n in range(lanes // width):
        out += jnp.where(block == n, square[n * width : (n + 1) * width, :], 0.0)
    return out


def tail_rows(block, chunks):
    return -(-(block * chunks) // 16) * 16


def masked_rows(panel, count):
    live = iota(panel.shape, 0) < count
    return jnp.where(live, panel.astype(F32), 0.0).astype(BF16)


def rounded(values):
    return values.astype(BF16)


def pack_kernel(block, width, chunks, panels, amps, count, out, held, amps_held, count_held, made, sems):
    first = lax.axis_index("aux") * block
    coming = [
        pltpu.make_async_copy(amps, amps_held, sems.at[0]),
        pltpu.make_async_copy(count, count_held, sems.at[1]),
    ]
    for j in range(block):
        coming.append(pltpu.make_async_copy(panels.at[first + j], held.at[j], sems.at[2 + j]))
    for copy in coming:
        copy.start()
    pao = held.shape[2]
    pairs = amps_held.shape[0]
    tail = tail_rows(block, chunks)
    row = iota((tail, pairs), 0)
    source = iota((tail, pairs), 1)
    hots = []
    for chunk in range(chunks):
        inside = (row >= chunk * block) & (row < (chunk + 1) * block)
        hots.append((inside & (source == first + row - chunk * block)).astype(F32).astype(BF16))
    going = []

    def send(start, rows):
        part = pl.ds(start, rows)
        sem = sems.at[2 + block + len(going)]
        going.append(pltpu.make_async_copy(made.at[part], out.at[part], sem))
        going[-1].start()

    coming[0].wait()
    rows = jnp.zeros((tail, pao), F32)
    for chunk, hot in enumerate(hots):
        rows += dot_nn(hot, amps_held[:, chunk * pao : (chunk + 1) * pao])
    made[block * width :, :] = rows.astype(BF16)
    send(block * width, tail)
    coming[1].wait()
    for j in range(block):
        coming[2 + j].wait()
        made[j * width : (j + 1) * width, :] = masked_rows(held[j], count_held[first + j])
        send(j * width, width)
    for copy in going:
        copy.wait()


def pack(panels, amps, count, block):
    pairs, width, pao = panels.shape
    chunks = width * width // pao
    rows = block * width + tail_rows(block, chunks)
    return pl.pallas_call(
        functools.partial(pack_kernel, block, width, chunks),
        out_shape=jax.ShapeDtypeStruct((rows, pao), BF16),
        in_specs=[whole(pltpu.HBM)] * 3,
        out_specs=whole(pltpu.HBM),
        scratch_shapes=[
            pltpu.VMEM((block, width, pao), BF16),
            pltpu.VMEM(amps.shape, BF16),
            pltpu.SMEM(count.shape, I32),
            pltpu.VMEM((rows, pao), BF16),
            pltpu.SemaphoreType.DMA((3 + 2 * block,)),
        ],
        compiler_params=pltpu.CompilerParams(vmem_limit_bytes=PACK_VMEM_BYTES),
        name="pack",
    )(panels, amps, count)


def local_kernel(
    block,
    width,
    ways,
    coupling,
    orbital,
    lmo,
    pos,
    fock,
    amps,
    energy,
    count,
    fit,
    panels,
    weight_in,
    weight_out,
    block_amps,
    own,
    masked,
    out,
    weight,
    fock_of,
    held,
    panels_held,
    count_held,
    both,
    sems,
):
    copies = [
        pltpu.make_async_copy(count, count_held, sems.at[0]),
        pltpu.make_async_copy(panels, panels_held, sems.at[1]),
    ]
    groups = fit.shape[0] // block
    fits = []
    for group in range(groups):
        part = pl.ds(group * block, block)
        fits.append(pltpu.make_async_copy(fit.at[part], held.at[part], sems.at[2 + group]))
    for copy in copies + fits:
        copy.start()
    total = pos.shape[1]
    occ = fock.shape[0]
    couplings = orbital.shape[0]
    per_dev = energy.shape[0]
    pair_devices = total // per_dev
    wide = per_dev * width
    thin = block * width
    functions = held.shape[2]
    pao = held.shape[3]
    pair = lax.axis_index("pair")
    first = lax.axis_index("aux") * block
    level = iota((occ, total), 0)
    hot_i = (lmo[0:1, :] == level).astype(F32)
    hot_j = (lmo[1:2, :] == level).astype(F32)

    def weights_of_targets():
        here = pos[...] == iota((total, total), 0)
        label_at = jnp.sum(jnp.where(here, iota((total, total), 1), 0), axis=1, keepdims=True)
        fock_of[0] = dot_nn(fock[...], hot_j, HIGHEST)
        fock_of[1] = lax.dot_general(
            fock[...], hot_i, (((0,), (0,)), ((), ())), precision=HIGHEST, preferred_element_type=F32
        )

        def add(c, value):
            hot_k = orbital[pl.ds(c, 1), :] == level
            for h in range(2):
                fock_k = jnp.sum(jnp.where(hot_k, fock_of[h], 0.0), axis=0, keepdims=True)
                named = coupling[pl.ds(2 * c + h, 1), :] == label_at
                value = value + jnp.where(named, fock_k, 0.0)
            return value

        if total <= 128:
            value = jnp.zeros((total, total), F32)
            for c in range(couplings):
                value = add(c, value)
            weight[...] = value
        else:
            weight[...] = jnp.zeros_like(weight)

            def step(c, carry):
                weight[...] = add(c, weight[...])
                return carry

            lax.fori_loop(0, couplings, step, 0)

    def spread_weights():
        def of_pairs(rows, start):
            hot = (iota((rows, total), 1) == start + iota((rows, total), 0)).astype(F32)
            return dot_nt(hot, weight[...], HIGHEST)

        wide_pair, _ = lane_in(width, wide)
        thin_pair, _ = lane_in(width, thin)
        mine = of_pairs(per_dev, pair * per_dev)
        local = (iota((total, wide), 0) == pair * per_dev + wide_pair).astype(F32)
        for k in range(len(ways) + 1):
            start = pair
            if k > 0:
                start = jnp.int32(-pair_devices)
                for sender, receiver in ways[k - 1]:
                    start = jnp.where(pair == receiver, sender, start)
            source = start * per_dev + first
            spread = (iota((total, thin), 0) == source + thin_pair).astype(F32)
            spread = dot_nn(mine, spread, HIGHEST)
            for group in range(groups):
                part = slice(group * block, (group + 1) * block)
                weight_in[k, group, :block, :] = spread[part, :]
            if k > 0:
                weight_out[k - 1] = dot_nn(of_pairs(8, source), local, HIGHEST)

    def amplitudes_and_energies():
        wide_pair, wide_pno = lane_in(width, wide)
        repeat = (iota((width, wide), 0) == wide_pno).astype(F32).astype(BF16)
        tiled = dot_nn(amps[...], repeat)
        row_pair, _ = row_in(width, wide)
        block_amps[...] = jnp.where(row_pair == wide_pair, tiled, 0.0).astype(BF16)
        across = iota((occ, occ), 0) == iota((occ, occ), 1)
        diagonal = jnp.sum(jnp.where(across, fock[...], 0.0), axis=1, keepdims=True)
        gap_of = jnp.sum((hot_i + hot_j) * diagonal, axis=0, keepdims=True)
        row = iota((width, width), 0)
        column = iota((width, width), 1)
        for j in range(block):
            at = iota((1, total), 1) == pair * per_dev + first + j
            gap = jnp.sum(jnp.where(at, gap_of, 0.0), axis=1, keepdims=True)
            flat = energy[pl.ds(first + j, 1), :]
            upright = jnp.sum(jnp.where(row == column, flat, 0.0), axis=1, keepdims=True)
            live = count_held[first + j]
            values = amps[pl.ds((first + j) * width, width), :].astype(F32)
            inside = (row < live) & (column < live)
            lanes = slice(j * width, (j + 1) * width)
            own[:, lanes] = jnp.where(inside, (upright + flat - gap) * values, 0.0)

    def masked_panels():
        for copy in copies:
            copy.wait()
        for p in range(per_dev):
            masked[p * width : (p + 1) * width, :] = masked_rows(panels_held[p], count_held[p])

    def exchange(group):
        for p in range(group * block, (group + 1) * block):
            rows = slice(p * width, (p + 1) * width)
            if functions % 128 == 0:
                fitted = dot_nt(masked[rows, :], held[p].reshape(2 * functions, pao)).astype(BF16)
                both[0, rows, :] = fitted[:, :functions]
                both[1, rows, :] = fitted[:, functions:]
            else:
                for h in range(2):
                    both[h, rows, :] = dot_nt(masked[rows, :], held[p, h]).astype(BF16)
        rows = slice(group * thin, (group + 1) * thin)
        out[group] = fold_diagonal(dot_nt(both[0, rows, :], both[1, rows, :]), width)

    beside = [weights_of_targets, spread_weights, amplitudes_and_energies]
    beside.pop(0)()
    beside.pop(0)()
    masked_panels()
    for group in range(groups):
        fits[group].wait()
        exchange(group)
        if beside:
            beside.pop(0)()
    for piece in beside:
        piece()


def local(coupling, orbital, lmo, pos, fock, amps, energy, count, fit, panels, block, ways):
    rounds = len(ways)
    wide, width = amps.shape
    per_dev, _, pao = panels.shape
    total = pos.shape[1]
    occ = fock.shape[0]
    groups = per_dev // block
    thin = block * width
    return pl.pallas_call(
        functools.partial(local_kernel, block, width, ways),
        out_shape=(
            jax.ShapeDtypeStruct((rounds + 1, groups, 8, thin), F32),
            jax.ShapeDtypeStruct((rounds, 8, wide), F32),
            jax.ShapeDtypeStruct((wide, wide), BF16),
            jax.ShapeDtypeStruct((width, thin), F32),
            jax.ShapeDtypeStruct((wide, pao), BF16),
            jax.ShapeDtypeStruct((groups, width, thin), F32),
        ),
        in_specs=[whole()] * 7 + [whole(pltpu.HBM)] * 3,
        out_specs=(whole(),) * 6,
        scratch_shapes=[
            pltpu.VMEM((total, total), F32),
            pltpu.VMEM((2, occ, total), F32),
            pltpu.VMEM(fit.shape, BF16),
            pltpu.VMEM(panels.shape, BF16),
            pltpu.SMEM(count.shape, I32),
            pltpu.VMEM((2, wide, fit.shape[2]), BF16),
            pltpu.SemaphoreType.DMA((2 + groups,)),
        ],
        compiler_params=pltpu.CompilerParams(vmem_limit_bytes=LOCAL_VMEM_BYTES),
        cost_estimate=pl.CostEstimate(
            flops=6_000_000_000, bytes_accessed=fit.size * 2, transcendentals=0
        ),
        name="local",
    )(coupling, orbital, lmo, pos, fock, amps, energy, count, fit, panels)


def unpack_amps(sent, block, width):
    thin = block * width
    pao = sent.shape[1]
    per_chunk = pao // width
    row_pair, row_pno = row_in(width, thin)
    row_chunk = floor_div(row_pno, per_chunk)
    tail = sent.shape[0] - thin
    pick = (iota((thin, tail), 1) == row_chunk * block + row_pair).astype(F32).astype(BF16)
    picked = dot_nn(pick, sent[thin:, :])
    lane_block, _ = lane_in(width, pao)
    at = row_pno - per_chunk * row_chunk == lane_block
    picked = jnp.where(at, picked, 0.0).astype(BF16)
    _, down_pno = row_in(width, pao)
    across_pair, across_pno = lane_in(width, thin)
    fold = (down_pno == across_pno).astype(F32).astype(BF16)
    return jnp.where(row_pair == across_pair, dot_nn(picked, fold), 0.0).astype(BF16)


def scaled(half, weight, width):
    rows = half.shape[0] // width
    return jnp.concatenate(
        [half[t * width : (t + 1) * width, :] * weight[t : t + 1, :] for t in range(rows)], 0
    )


def add_in(block, width, masked, parts, put):
    thin = block * width
    inters, halves = [], []
    for sent, _ in parts:
        inter = dot_nt(masked[...], sent[:thin, :]).astype(BF16)
        half = dot_nn(inter, unpack_amps(sent, block, width)).astype(BF16).astype(F32)
        inters.append(inter)
        halves.append(half)
    for group in range(masked.shape[0] // thin):
        rows = slice(group * thin, (group + 1) * thin)
        square = jnp.zeros((thin, thin), F32)
        for (_, weight_in), inter, half in zip(parts, inters, halves):
            high = rounded(scaled(half[rows, :], weight_in[group], width))
            square += dot_nt(high, inter[rows, :])
        put(group, fold_diagonal(square, width))


def add_in_two(block, width, masked, sent, amps, weight_in, away):
    thin = block * width
    aux = lax.axis_index("aux")
    odd = lax.bitwise_and(aux, 1)
    base = lax.bitwise_xor(aux, away) - odd
    rows = pl.ds(pl.multiple_of(base * thin, thin), 2 * thin)
    inter = dot_nt(masked[rows, :], sent[:thin, :]).astype(BF16)
    half = dot_nn(inter, amps).astype(BF16).astype(F32)
    added = []
    for n in range(2):
        part = slice(n * thin, (n + 1) * thin)
        high = rounded(scaled(half[part, :], weight_in[base + n], width))
        square = dot_nt(high, inter[part, :])
        added.append(fold_diagonal(square, width))
    first, second = added
    return jnp.where(odd == 0, first, second), jnp.where(odd == 0, second, first)


def add_back(block, width, sent, masked, block_amps, weight_out):
    thin = block * width
    inter = dot_nt(sent[:thin, :], masked[...]).astype(BF16)
    half = dot_nn(inter, block_amps[...]).astype(BF16).astype(F32)
    high = rounded(scaled(half, weight_out, width))
    return fold_diagonal(dot_nt(high, inter), width)


def both_kernel(block, width, *refs):
    masked, block_amps, acc, sent, weight_in, weight_out = refs[:6]
    out, back = refs[-2:]
    parts = [(sent, weight_in)] + ([refs[6:8]] if len(refs) > 8 else [])

    def put(group, value):
        out[group] = acc[group] - value

    back[...] = as_sent(add_back(block, width, sent, masked, block_amps, weight_out)).astype(BF16)
    add_in(block, width, masked, parts, put)


NEAR = 2


def far_kernel(block, width, sent, masked, block_amps, weight_out, weight_in, acc, back, *outs):
    amps = unpack_amps(sent, block, width)
    aux = lax.axis_index("aux")
    back[...] = as_sent(add_back(block, width, sent, masked, block_amps, weight_out)).astype(BF16)
    for k in range(0, len(outs), 2):
        added = add_in_two(block, width, masked, sent, amps, weight_in, NEAR + k)
        for n in range(2):
            group = lax.bitwise_xor(aux, NEAR + k + n)
            outs[k + n][...] = as_sent(acc[group] - added[n]).astype(BF16)


def near_kernel(block, width, returned, sent, masked, weight_in, acc, own, *refs):
    backs, outs = refs[:returned], refs[returned:]
    amps = unpack_amps(sent, block, width)
    aux = lax.axis_index("aux")
    added = add_in_two(block, width, masked, sent, amps, weight_in, 0)
    mine = as_sent(acc[aux] - added[0] + own[...])
    for back in backs:
        mine -= back[...].astype(F32)
    outs[0][...] = mine
    outs[1][...] = as_sent(acc[lax.bitwise_xor(aux, 1)] - added[1]).astype(BF16)


def finish_kernel(block, width, count, *refs):
    parts, out, held = refs[:count], refs[count], refs[count + 1]
    total = parts[0][...]
    for n, part in enumerate(parts[1:]):
        value = part[...].astype(F32)
        total = total - value if n == 0 else total + value
    for s in range(block):
        for r in range(0, width, 16):
            lane = r // 16 * block * width + s * width
            held[s * width + r : s * width + r + 16, :] = total[:, lane : lane + width]
    for a in range(width):
        out[:, a * width : (a + 1) * width] = held[pl.ds(a, block, stride=width), :]


def as_sent(values):
    rows = values.shape[0]
    return jnp.concatenate([values[r : r + 16, :] for r in range(0, rows, 16)], 1)


def call(kernel, name, out_shape, args, flops, scratch=()):
    many = isinstance(out_shape, tuple)
    return pl.pallas_call(
        kernel,
        out_shape=out_shape,
        in_specs=[whole()] * len(args),
        out_specs=(whole(),) * len(out_shape) if many else whole(),
        scratch_shapes=list(scratch),
        compiler_params=pltpu.CompilerParams(vmem_limit_bytes=VMEM_BYTES),
        cost_estimate=pl.CostEstimate(flops=flops, bytes_accessed=3_000_000, transcendentals=0),
        name=name,
    )(*args)


def schedule(devices):
    if devices == 4:
        return [[(0, 2), (3, 1), (2, 3), (1, 0)], [(1, 2), (3, 0)]]
    rounds = []
    for k in range(1, devices // 2 + 1):
        whole_way = [(p, (p + k) % devices) for p in range(devices)]
        if 2 * k == devices:
            whole_way = [way for way in whole_way if (way[0] < k) == (way[0] % 2 == 0)]
        rounds.append(whole_way)
    return rounds


def completed(way, devices):
    idle = sorted(set(range(devices)) - {p for p, _ in way})
    open_ends = sorted(set(range(devices)) - {q for _, q in way})
    return way + list(zip(idle, open_ends))


def on_device(
    panels,
    amplitudes,
    fitted_ints,
    pno_energy,
    fock_occ,
    pno_count,
    pair_pos,
    coupling,
    coupling_lmo,
    pair_lmo,
):
    per_dev, width, pao = panels.shape
    pair_devices = lax.axis_size("pair")
    aux_devices = lax.axis_size("aux")
    block = per_dev // aux_devices
    thin = block * width
    couplings = coupling.shape[1]
    total = pair_pos.shape[0]
    ways = schedule(pair_devices)
    rounds = len(ways)
    back_ways = [completed([(q, p) for p, q in way], pair_devices) for way in ways]

    sent = pack(panels, amplitudes, pno_count, block)
    arrived = [lax.ppermute(sent, "pair", way) for way in ways]
    weight_in, weight_out, block_amps, own, masked, acc = local(
        coupling.transpose(1, 2, 0).reshape(2 * couplings, total),
        coupling_lmo.T,
        pair_lmo.T,
        pair_pos[None, :],
        fock_occ,
        amplitudes.reshape(per_dev * width, width),
        pno_energy,
        pno_count,
        fitted_ints,
        panels,
        block,
        ways,
    )

    acc_shape = jax.ShapeDtypeStruct(acc.shape, F32)
    own_shape = jax.ShapeDtypeStruct((16, width // 16 * thin), F32)
    block_shape = jax.ShapeDtypeStruct(own_shape.shape, BF16)
    flops = 1_000_000_000
    returned = []
    for k in range(1, rounds):
        args = (masked, block_amps, acc, arrived[k - 1], weight_in[k], weight_out[k - 1])
        if k == 1:
            args += (sent, weight_in[0])
        acc, back = call(
            functools.partial(both_kernel, block, width),
            "couple",
            (acc_shape, block_shape),
            args,
            2 * flops,
        )
        returned.append(lax.ppermute(back, "pair", back_ways[k - 1]))
    back, *far = call(
        functools.partial(far_kernel, block, width),
        "couple_far",
        (block_shape,) * (1 + aux_devices - NEAR),
        (arrived[-1], masked, block_amps, weight_out[-1], weight_in[rounds], acc),
        flops,
    )
    last_back = lax.ppermute(back, "pair", back_ways[-1])
    near = call(
        functools.partial(near_kernel, block, width, len(returned)),
        "couple_near",
        (own_shape,) + (block_shape,) * (NEAR - 1),
        (arrived[-1], masked, weight_in[rounds], acc, own, *returned),
        flops,
    )
    parts = list(near) + far
    sums = {0: last_back}
    for k in range(1, aux_devices):
        sums[k] = lax.ppermute(parts[k], "aux", [(d, d ^ k) for d in range(aux_devices)])
    order = [0, 3, 2]
    order += [k for k in range(1, aux_devices) if k not in order]
    sums = [parts[0]] + [sums[k] for k in order]
    return call(
        functools.partial(finish_kernel, block, width, len(sums)),
        "finish",
        jax.ShapeDtypeStruct((block, width * width), F32),
        tuple(sums),
        1_000_000,
        [pltpu.VMEM((thin, width), F32)],
    )


def solution(mesh):
    placed = (
        P(("groups", "pair"), None, None),
        P(("groups", "pair"), None),
        P(("groups", "pair"), None, "aux", None),
        P(("groups", "pair"), None),
        P("groups", None),
        P(("groups", "pair")),
        P("groups"),
        P("groups", None, None),
        P("groups", None),
        P("groups", None),
    )
    return jax.shard_map(
        on_device,
        mesh=mesh,
        in_specs=placed,
        out_specs=P(("groups", "pair", "aux"), None),
        check_vma=False,
    )
```
